256 devices in a mesh: fsdp: 64 (over y, z, core), rep: 4 (over x).
Axes of the slice: x: 4, y: 4, z: 8, core: 2. Of those that a mesh axis runs over, the one named last changes fastest.
Arguments:
- grad_parts: bfloat16 [4, 80, 1024, 1024], P('rep', None, 'fsdp'), may hold values from -6 to 6
- moment: float32 [80, 1024, 1024], P(None, 'fsdp', 'rep'), may hold values from 0.001 to 3000, as said below
- owner: int32 [80], replicated, may hold values from 0 to 63, as said below
- left_root: bfloat16 [64, 3, 1024, 1024], P('fsdp'), may hold values from -0.5 to 2.02, as said below
- right_root: bfloat16 [64, 3, 1024, 1024], P('fsdp', None, None, 'rep'), may hold values from -0.5 to 2.02, as said below
Outputs:
- update: float32 [80, 1024, 1024], P(None, 'fsdp', 'rep')
The draws below stay inside these ranges and needn't reach their ends.
Inputs may be any that keep to these rules, and one draw needn't show every extreme that they name: `owner`: no fsdp index owns more than 3 blocks, and in every draw one index owns exactly 3. `left_root`: positive on the diagonal. Slot s of owner o holds the factor of the s-th block (in increasing block order) that o owns; other slots are unused. `right_root`: positive on the diagonal. Slots as for left_root. `moment`: Positive.
All inputs are finite; a program needn't handle non-finite values.
Results may differ from the reference program's by a relative error of at most 0.017.
Values may be sent and summed in bfloat16 or wider, within the bound.
No kernel may reach another device: no remote copies, remote signals or barrier semaphores. Data moves between devices by JAX's collectives and lax.ppermute only.
A program may use at most 128 MiB of HBM per device.

```python
import math
import jax
import jax.numpy as jnp
from jax import lax

BLOCK = 1024
BLOCKS = 80
CAP = 3
REPLICAS = 4
N_FSDP = 64


def root_factor(key, diagonal):
    noise = jax.random.normal(key, (N_FSDP, CAP, BLOCK, BLOCK), jnp.float32)
    symmetric = (noise + jnp.swapaxes(noise, 2, 3)) * (0.3 / math.sqrt(BLOCK))
    numbers = jnp.arange(BLOCK)
    on_diagonal = numbers[:, None] == numbers[None, :]
    return jnp.where(on_diagonal, diagonal[:, :, :, None], symmetric)


def draw_left_root(key, part):
    key = jax.random.fold_in(key, 7)
    first, later = jax.random.split(key)
    diagonal = jnp.exp(jax.random.uniform(first, (N_FSDP, CAP, BLOCK), jnp.float32, -0.7, 0.7))
    return root_factor(later, diagonal).astype(jnp.bfloat16)


def draw_right_root(key, part):
    key = jax.random.fold_in(key, 9)
    first, later = jax.random.split(key)
    diagonal = jnp.exp(jax.random.uniform(first, (N_FSDP, CAP, BLOCK), jnp.float32, -0.7, 0.7))
    return root_factor(later, diagonal).astype(jnp.bfloat16)


def draw_moment(key, part):
    key = jax.random.fold_in(key, 5)
    first, middle, last = jax.random.split(key, 3)
    rows = jnp.arange(BLOCK, dtype=jnp.float32) / (BLOCK - 1)
    row_scale = jnp.exp(-2.0 * math.log(10.0) * rows)
    column_scale = jnp.exp(jax.random.uniform(first, (BLOCKS, 1, BLOCK), jnp.float32, 0.0, 2.0 * math.log(10.0)))
    base = jnp.exp(jax.random.uniform(middle, (BLOCKS, BLOCK, BLOCK), jnp.float32, -0.7, 0.7))
    block_scale = jnp.exp(jax.random.uniform(last, (BLOCKS, 1, 1), jnp.float32, -1.15, 1.15))
    return 4.0 * base * block_scale * column_scale * row_scale[None, :, None]


def draw_owner(key, part):
    key = jax.random.fold_in(key, 11)
    first, middle, last = jax.random.split(key, 3)
    places = jax.random.permutation(first, N_FSDP * CAP).astype(jnp.int32)
    chosen = jax.random.randint(middle, (), 0, N_FSDP).astype(jnp.int32)
    position = jnp.arange(N_FSDP * CAP, dtype=jnp.int32)
    score = jnp.where(places // CAP == chosen, position - N_FSDP * CAP, position)
    order = jnp.argsort(score, stable=True)
    owners = (places[order][:BLOCKS] // CAP).astype(jnp.int32)
    shuffle = jax.random.permutation(last, BLOCKS)
    return owners[shuffle].astype(jnp.int32)


def shard_levels(rng, extent, pieces, smallest, high):
    def one(axis_at, shards_of):
        heights = jax.random.uniform(jax.random.fold_in(jax.random.fold_in(rng, 6), axis_at), (shards_of,), jnp.float32, smallest / len(pieces), high / len(pieces))
        return jnp.repeat(jnp.exp(heights), extent[axis_at] // shards_of).reshape((-1,) + (1,) * (len(extent) - axis_at - 1))

    loudness = one(*pieces[0])
    for cut in pieces[1:]:
        loudness = loudness * one(*cut)
    return loudness


def bell_draw(key, extent, deviation, reach, shards=(), kind=jnp.bfloat16):
    gain = shard_levels(key, extent, shards, -0.22, 0.18) if shards else 1.0
    result = jax.random.normal(key, extent, jnp.float32) * deviation * gain
    return jnp.minimum(jnp.maximum(result, -reach), reach).astype(kind)


def setup_inputs(seed: int = 0) -> dict:
    splits = jax.random.split(jax.random.key(seed), 6)
    grad_parts = bell_draw(splits[0], (REPLICAS, BLOCKS, BLOCK, BLOCK), 1.0, 6.0, ((0, 4), (2, 64)))
    moment = draw_moment(jax.random.fold_in(splits[5], 71), 0)
    owner = draw_owner(jax.random.fold_in(splits[5], 71), 0)
    left_root = draw_left_root(jax.random.fold_in(splits[5], 71), 0)
    right_root = draw_right_root(jax.random.fold_in(splits[5], 71), 0)
    return dict(grad_parts=grad_parts, moment=moment, owner=owner, left_root=left_root, right_root=right_root)


second_decay = 0.99
adam_epsilon = 1e-08
norm_epsilon = 1e-06

def block_slots(owner):
    count = owner.shape[0]
    numbers = jnp.arange(count, dtype=jnp.int32)
    same = owner[:, None] == owner[None, :]
    earlier = numbers[None, :] < numbers[:, None]
    return lax.optimization_barrier(jnp.sum(jnp.where(same & earlier, 1, 0), axis=1)).astype(jnp.int32)

def reference(grad_parts, moment, owner, left_root, right_root):
    gradient = lax.optimization_barrier(jnp.sum(grad_parts.astype(jnp.float32), axis=0))
    second = second_decay * moment + (1.0 - second_decay) * gradient * gradient
    adam_direction = gradient / (jnp.sqrt(second) + adam_epsilon)
    adam_norm = jnp.sqrt(lax.optimization_barrier(jnp.sum(adam_direction * adam_direction, axis=(1, 2))))
    gradient_low = gradient.astype(jnp.bfloat16)
    slot = block_slots(owner)

    def precondition(index):
        chosen = owner[index]
        place = slot[index]
        right = right_root[chosen, place].astype(jnp.float32)
        left = left_root[chosen, place].astype(jnp.float32)
        inner = jnp.dot(gradient_low[index].astype(jnp.float32), right, preferred_element_type=jnp.float32, precision=lax.Precision.HIGHEST)
        inner_low = lax.optimization_barrier(inner.astype(jnp.bfloat16))
        product = jnp.dot(left, inner_low.astype(jnp.float32), preferred_element_type=jnp.float32, precision=lax.Precision.HIGHEST)
        return product.astype(jnp.bfloat16)
    shampoo = lax.map(precondition, jnp.arange(owner.shape[0], dtype=jnp.int32))
    shampoo_wide = shampoo.astype(jnp.float32)
    shampoo_norm = jnp.sqrt(lax.optimization_barrier(jnp.sum(shampoo_wide * shampoo_wide, axis=(1, 2))))
    ratio = adam_norm / (shampoo_norm + norm_epsilon)
    return shampoo_wide * ratio[:, None, None]
```

```python
import jax
import jax.numpy as jnp
from jax import lax
from jax.experimental import pallas as pl
from jax.experimental.pallas import tpu as pltpu
from jax.sharding import PartitionSpec as P

second_decay = 0.99
adam_epsilon = 1e-08
norm_epsilon = 1e-06

REP = 4
OWNERS = 64
CAP = 3
VMEM = pl.BlockSpec(memory_space=pltpu.VMEM)
SMEM = pl.BlockSpec(memory_space=pltpu.SMEM)
ROOM = 48 * 1024 * 1024


def block_slots(owner):
    count = owner.shape[0]
    numbers = jnp.arange(count, dtype=jnp.int32)
    same = owner[:, None] == owner[None, :]
    earlier = numbers[None, :] < numbers[:, None]
    return jnp.sum(jnp.where(same & earlier, 1, 0), axis=1).astype(jnp.int32)


def shift(value, step):
    return lax.ppermute(value, "rep", [(i, (i + step) % REP) for i in range(REP)])


def wide(value):
    return value.astype(jnp.float32)


def sum_over_rep(pieces):
    middle = pieces[0].shape[0] // 2
    top, bottom = slice(0, middle), slice(middle, None)
    far_right = shift(pieces[2][top], 1)
    far_left = shift(pieces[2][bottom], 3)
    near_right = shift(pieces[1][bottom], 1)
    near_left = shift(pieces[3][top], 3)
    on_right = (wide(pieces[1][top]) + wide(far_right)).astype(jnp.bfloat16)
    on_left = (wide(pieces[3][bottom]) + wide(far_left)).astype(jnp.bfloat16)
    last_right = shift(on_right, 1)
    last_left = shift(on_left, 3)
    return (pieces[0], near_left, last_right, near_right, last_left), (on_right, on_left)


def gather_over_rep(value):
    middle = value.shape[1] // 2
    top, bottom = value[:, :middle], value[:, middle:]
    left_top = shift(top, 1)
    right_bottom = shift(bottom, 3)
    left_bottom = shift(bottom, 1)
    right_top = shift(top, 3)
    far_top = shift(left_top, 1)
    far_bottom = shift(right_bottom, 3)
    return value, left_top, left_bottom, far_top, far_bottom, right_top, right_bottom


def sum_pack_kernel(source, own, near_left, last_right, near_right, last_left, low, out):
    middle = near_left.shape[0]

    @pl.loop(0, middle)
    def _(b):
        low[b] = (wide(own[b]) + (wide(near_left[b]) + wide(last_right[b]))).astype(jnp.bfloat16)
        c = middle + b
        low[c] = (wide(own[c]) + (wide(near_right[b]) + wide(last_left[b]))).astype(jnp.bfloat16)

    @pl.loop(0, OWNERS)
    def _(o):
        for s in range(CAP):
            out[o, s] = low[source[s * OWNERS + o]]


def sum_pack(source, terms):
    blocks, rows, columns = terms[0].shape
    return pl.pallas_call(
        sum_pack_kernel,
        out_shape=[
            jax.ShapeDtypeStruct((blocks, rows, columns), jnp.bfloat16),
            jax.ShapeDtypeStruct((OWNERS, CAP, rows, columns), jnp.bfloat16),
        ],
        in_specs=[SMEM] + [VMEM] * 5,
        out_specs=[VMEM, VMEM],
        compiler_params=pltpu.CompilerParams(vmem_limit_bytes=ROOM),
        name="sum_pack",
    )(source, *terms)


def left_kernel(first, place, gradient, left, out, wide_rows):
    halves, size, half = wide_rows.shape
    width = halves * half
    rows = gradient.shape[2]
    part = rows // REP
    s = pl.program_id(0)
    low = gradient[:, first + s].reshape(size, width)
    tile = size // 4
    for i in range(4):
        at = slice(i * tile, (i + 1) * tile)
        product = jnp.dot(left[0, at, :], low, preferred_element_type=jnp.float32)
        for h in range(halves):
            wide_rows[h, at, :] = product[:, h * half : (h + 1) * half]
    for target in range(REP):
        k = lax.rem(target + REP - place[0], REP)
        for j in range(part):
            for h in range(halves):
                strided = wide_rows[h, pl.ds(target * part + j, OWNERS, stride=rows), :]
                at = slice(j * OWNERS, (j + 1) * OWNERS), slice(h * half, (h + 1) * half)
                out[(k, 0) + at] = strided.astype(jnp.bfloat16)


def left_multiply(place, gradient, left, first, count):
    size, width = left.shape[1], gradient.shape[3]
    return pl.pallas_call(
        lambda *refs: left_kernel(first, *refs),
        grid=(count,),
        out_shape=jax.ShapeDtypeStruct((REP, count, size // REP, width), jnp.bfloat16),
        in_specs=[SMEM, VMEM, pl.BlockSpec((1, size, size), lambda i: (first + i, 0, 0))],
        out_specs=pl.BlockSpec((REP, 1, size // REP, width), lambda i: (0, i, 0, 0)),
        scratch_shapes=[pltpu.VMEM((width // 128, size, 128), jnp.float32)],
        compiler_params=pltpu.CompilerParams(vmem_limit_bytes=ROOM),
        cost_estimate=pl.CostEstimate(
            flops=count * 2 * size * size * width,
            bytes_accessed=count * 4 * size * size,
            transcendentals=0,
        ),
        name="left_multiply",
    )(place, gradient, left)


def right_kernel(place, *refs):
    pieces, rights = refs[:REP], refs[REP : REP + 7]
    out, total, full, wide_rows = refs[REP + 7 :]
    height, size = full.shape
    width = size // REP
    halves, _, half = wide_rows.shape
    rows = out.shape[2]
    part = rows // REP
    for k, piece in enumerate(pieces):
        at = pl.multiple_of(lax.rem(place[0] + (REP - k), REP) * width, width)
        full[:, pl.ds(at, width)] = piece[0]
    squares = jnp.zeros((8, width), jnp.float32)
    middle = size // 2
    for k in range(REP):
        if k == 0:
            product = jnp.dot(full[...], rights[0][0], preferred_element_type=jnp.float32)
        else:
            top, bottom = rights[2 * k - 1], rights[2 * k]
            product = jnp.dot(full[:, :middle], top[0], preferred_element_type=jnp.float32)
            product = product + jnp.dot(
                full[:, middle:], bottom[0], preferred_element_type=jnp.float32
            )
        squares = squares + jnp.sum((product * product).reshape(height // 8, 8, width), axis=0)
        for j in range(part):
            for h in range(halves):
                wide_rows[h, pl.ds(k * part + j, OWNERS, stride=rows), :] = product[
                    j * OWNERS : (j + 1) * OWNERS, h * half : (h + 1) * half
                ]
    for h in range(halves):
        low = wide_rows[h].astype(jnp.bfloat16).reshape(OWNERS, rows, half)
        out[:, 0, :, h * half : (h + 1) * half] = low
    total[0] = jnp.sum(squares, axis=0, keepdims=True)


def right_multiply(place, pieces, rights):
    count, height, width = pieces[0].shape
    size = rights[0].shape[1]
    rows = size // OWNERS
    return pl.pallas_call(
        right_kernel,
        grid=(count,),
        out_shape=[
            jax.ShapeDtypeStruct((OWNERS, count, rows, width), jnp.bfloat16),
            jax.ShapeDtypeStruct((count, 1, width), jnp.float32),
        ],
        in_specs=[SMEM]
        + [pl.BlockSpec((1, height, width), lambda i: (i, 0, 0))] * 4
        + [pl.BlockSpec((1,) + r.shape[1:], lambda i: (i, 0, 0)) for r in rights],
        out_specs=[
            pl.BlockSpec((OWNERS, 1, rows, width), lambda i: (0, i, 0, 0)),
            pl.BlockSpec((1, 1, width), lambda i: (i, 0, 0)),
        ],
        scratch_shapes=[
            pltpu.VMEM((height, size), jnp.bfloat16),
            pltpu.VMEM((width // 128, size, 128), jnp.float32),
        ],
        compiler_params=pltpu.CompilerParams(vmem_limit_bytes=ROOM),
        cost_estimate=pl.CostEstimate(
            flops=count * 2 * size * size * width,
            bytes_accessed=count * 4 * size * size,
            transcendentals=0,
        ),
        name="right_multiply",
    )(place, *pieces, *rights)


def split_kernel(owner, slot, back01, back2, out, held):
    _, groups, rows, _ = out.shape
    part = rows // REP

    held[:, :2] = back01[...]
    held[:, 2] = back2[:, 0]

    @pl.loop(0, groups)
    def _(g):
        parts = []
        for i in range(REP):
            b = g * REP + i
            parts.append(wide(held[owner[b], slot[b]]))
        for k in range(REP):
            joined = [p[k * part : (k + 1) * part] for p in parts]
            out[(REP - k) % REP, g] = jnp.concatenate(joined, axis=0).astype(jnp.bfloat16)


def split_blocks(owner, slot, back01, back2):
    blocks = owner.shape[0]
    _, _, rows, width = back01.shape
    return pl.pallas_call(
        split_kernel,
        out_shape=jax.ShapeDtypeStruct((REP, blocks // REP, rows, width), jnp.bfloat16),
        in_specs=[SMEM] * 2 + [VMEM] * 2,
        out_specs=VMEM,
        scratch_shapes=[pltpu.VMEM((OWNERS, CAP, rows, width), jnp.bfloat16)],
        compiler_params=pltpu.CompilerParams(vmem_limit_bytes=ROOM),
        name="split_blocks",
    )(owner, slot, back01, back2)


def join_kernel(place, ratio, own, first, second, third, out, held):
    groups, rows, _ = own.shape
    part = rows // REP
    for k, piece in enumerate((own, first, second, third)):
        held[lax.rem(place[0] + (REP - k), REP)] = piece[...]

    @pl.loop(0, groups)
    def _(g):
        parts = [wide(held[q, g]) for q in range(REP)]
        for i in range(REP):
            joined = [p[i * part : (i + 1) * part] for p in parts]
            out[g * REP + i] = jnp.concatenate(joined, axis=0) * ratio[g * REP + i]


def join_blocks(place, ratio, pieces):
    groups, rows, width = pieces[0].shape
    return pl.pallas_call(
        join_kernel,
        out_shape=jax.ShapeDtypeStruct((groups * REP, rows, width), jnp.float32),
        in_specs=[SMEM] * 2 + [VMEM] * 4,
        out_specs=VMEM,
        scratch_shapes=[pltpu.VMEM((REP, groups, rows, width), jnp.bfloat16)],
        compiler_params=pltpu.CompilerParams(vmem_limit_bytes=ROOM),
        name="join_blocks",
    )(place, ratio, *pieces)


def adam_squares(low, moment):
    gradient = wide(low)
    second = second_decay * moment + (1.0 - second_decay) * gradient * gradient
    direction = gradient / (jnp.sqrt(second) + adam_epsilon)
    return jnp.sum(direction * direction, axis=(1, 2))


def exchange(value):
    return lax.all_to_all(value, "fsdp", split_axis=0, concat_axis=0)


def after(value, *others):
    return lax.optimization_barrier((value, *others))[0]


def shards(grad_parts, moment, owner, left_root, right_root):
    place = lax.axis_index("rep")
    place_ref = place.astype(jnp.int32).reshape(1)
    blocks, rows, columns = moment.shape
    slot = block_slots(owner)
    numbers = jnp.arange(blocks, dtype=jnp.int32)
    target = slot * OWNERS + owner
    places = jnp.arange(OWNERS * CAP, dtype=jnp.int32)
    matched = places[:, None] == target[None, :]
    source = jnp.sum(jnp.where(matched, numbers[None, :], 0), axis=1)
    gradient = grad_parts[0]
    pieces = [
        lax.dynamic_slice(
            gradient, (0, 0, lax.rem(place + k, REP) * columns), (blocks, rows, columns)
        )
        for k in range(REP)
    ]
    terms, passing = sum_over_rep(pieces)
    rights01 = gather_over_rep(after(right_root[0, :2], *passing))
    low, packed = sum_pack(source, terms)
    owned = exchange(packed)
    adam = lax.psum(adam_squares(low, moment), "rep")

    def spread(sent):
        return [sent[0]] + [shift(sent[k], k) for k in (1, 2, 3)]

    sent01 = left_multiply(after(place_ref, *rights01), owned, left_root[0], 0, 2)
    held01 = spread(sent01)
    result01, square01 = right_multiply(place_ref, held01, rights01)
    back01 = exchange(result01)
    rights2 = gather_over_rep(after(right_root[0, 2:], *held01))
    sent2 = left_multiply(after(place_ref, *held01), owned, left_root[0], 2, 1)
    held2 = spread(sent2)
    result2, square2 = right_multiply(place_ref, held2, rights2)
    back2 = exchange(after(result2, back01))
    squares = lax.psum(jnp.sum(jnp.concatenate([square01, square2]), axis=(1, 2)), "rep")
    known = jnp.concatenate([adam, squares, jnp.zeros((128 - blocks - CAP,), jnp.float32)])
    known = jnp.broadcast_to(known[None, None, :], (OWNERS, 1, 128))
    sent = split_blocks(owner, slot, back01, back2)
    known = exchange(after(known, sent))[:, 0]
    adam_norm = jnp.sqrt(jnp.sum(known[:, :blocks], axis=0))
    by_place = jnp.transpose(known[:, blocks : blocks + CAP]).reshape(OWNERS * CAP, 1)
    shampoo_norm = jnp.sqrt(jnp.sum(jnp.where(matched, by_place, 0.0), axis=0))
    ratio = adam_norm / (shampoo_norm + norm_epsilon)
    held = spread(sent)
    return join_blocks(place_ref, ratio, held)


def solution(mesh):
    in_specs = (
        P("rep", None, "fsdp", None),
        P(None, "fsdp", "rep"),
        P(),
        P("fsdp", None, None, None),
        P("fsdp", None, None, "rep"),
    )
    out_specs = P(None, "fsdp", "rep")
    return jax.shard_map(shards, mesh=mesh, in_specs=in_specs, out_specs=out_specs, check_vma=False)
```

```python
import jax
import jax.numpy as jnp
from jax import lax
from jax.experimental import pallas as pl
from jax.experimental.pallas import tpu as pltpu
from jax.sharding import PartitionSpec as P

second_decay = 0.99
adam_epsilon = 1e-08
norm_epsilon = 1e-06

REP = 4
OWNERS = 64
CAP = 3
VMEM = pl.BlockSpec(memory_space=pltpu.VMEM)
SMEM = pl.BlockSpec(memory_space=pltpu.SMEM)
ROOM = 48 * 1024 * 1024


def block_slots(owner):
    count = owner.shape[0]
    numbers = jnp.arange(count, dtype=jnp.int32)
    same = owner[:, None] == owner[None, :]
    earlier = numbers[None, :] < numbers[:, None]
    return jnp.sum(jnp.where(same & earlier, 1, 0), axis=1).astype(jnp.int32)


def shift(value, step):
    return lax.ppermute(value, "rep", [(i, (i + step) % REP) for i in range(REP)])


def wide(value):
    return value.astype(jnp.float32)


def sum_over_rep(pieces):
    middle = pieces[0].shape[0] // 2
    top, bottom = slice(0, middle), slice(middle, None)
    far_right = shift(pieces[2][top], 1)
    far_left = shift(pieces[2][bottom], 3)
    near_right = shift(pieces[1][bottom], 1)
    near_left = shift(pieces[3][top], 3)
    on_right = (wide(pieces[1][top]) + wide(far_right)).astype(jnp.bfloat16)
    on_left = (wide(pieces[3][bottom]) + wide(far_left)).astype(jnp.bfloat16)
    last_right = shift(on_right, 1)
    last_left = shift(on_left, 3)
    return (pieces[0], near_left, last_right, near_right, last_left), (on_right, on_left)


def gather_over_rep(value, *others):
    middle = value.shape[1] // 2
    top, bottom = after((value[:, :middle], value[:, middle:]), *others)
    left_top = shift(top, 1)
    right_bottom = shift(bottom, 3)
    left_bottom = shift(bottom, 1)
    right_top = shift(top, 3)
    far_top = shift(left_top, 1)
    far_bottom = shift(right_bottom, 3)
    return value, left_top, left_bottom, far_top, far_bottom, right_top, right_bottom


def near(gathered):
    return gathered[1], gathered[2], gathered[5], gathered[6]


def sum_pack_kernel(
    source, own, near_left, last_right, near_right, last_left, low, out01, out2
):
    middle = near_left.shape[0]

    @pl.loop(0, middle)
    def _(b):
        low[b] = (wide(own[b]) + (wide(near_left[b]) + wide(last_right[b]))).astype(jnp.bfloat16)
        c = middle + b
        low[c] = (wide(own[c]) + (wide(near_right[b]) + wide(last_left[b]))).astype(jnp.bfloat16)

    @pl.loop(0, OWNERS)
    def _(o):
        out01[o, 0] = low[source[o]]
        out01[o, 1] = low[source[OWNERS + o]]
        out2[o, 0] = low[source[2 * OWNERS + o]]


def sum_pack(source, terms):
    blocks, rows, columns = terms[0].shape
    return pl.pallas_call(
        sum_pack_kernel,
        out_shape=[
            jax.ShapeDtypeStruct((blocks, rows, columns), jnp.bfloat16),
            jax.ShapeDtypeStruct((OWNERS, 2, rows, columns), jnp.bfloat16),
            jax.ShapeDtypeStruct((OWNERS, 1, rows, columns), jnp.bfloat16),
        ],
        in_specs=[SMEM] + [VMEM] * 5,
        out_specs=[VMEM] * 3,
        compiler_params=pltpu.CompilerParams(vmem_limit_bytes=ROOM),
        name="sum_pack",
    )(source, *terms)


def left_kernel(place, gradient, left, out, wide_rows):
    halves, size, half = wide_rows.shape
    width = halves * half
    rows = gradient.shape[2]
    part = rows // REP
    s = pl.program_id(0)
    low = gradient[:, s].reshape(size, width)
    tile = size // 4
    for i in range(4):
        at = slice(i * tile, (i + 1) * tile)
        product = jnp.dot(left[0, at, :], low, preferred_element_type=jnp.float32)
        for h in range(halves):
            wide_rows[h, at, :] = product[:, h * half : (h + 1) * half]
    for target in range(REP):
        k = lax.rem(target + REP - place[0], REP)
        for j in range(part):
            for h in range(halves):
                strided = wide_rows[h, pl.ds(target * part + j, OWNERS, stride=rows), :]
                at = slice(j * OWNERS, (j + 1) * OWNERS), slice(h * half, (h + 1) * half)
                out[(k, 0) + at] = strided.astype(jnp.bfloat16)


def left_multiply(place, gradient, left, first):
    size, width = left.shape[1], gradient.shape[3]
    count = gradient.shape[1]
    return pl.pallas_call(
        left_kernel,
        grid=(count,),
        out_shape=jax.ShapeDtypeStruct((REP, count, size // REP, width), jnp.bfloat16),
        in_specs=[SMEM, VMEM, pl.BlockSpec((1, size, size), lambda i: (first + i, 0, 0))],
        out_specs=pl.BlockSpec((REP, 1, size // REP, width), lambda i: (0, i, 0, 0)),
        scratch_shapes=[pltpu.VMEM((width // 128, size, 128), jnp.float32)],
        compiler_params=pltpu.CompilerParams(vmem_limit_bytes=ROOM),
        cost_estimate=pl.CostEstimate(
            flops=count * 2 * size * size * width,
            bytes_accessed=count * 4 * size * size,
            transcendentals=0,
        ),
        name="left_multiply",
    )(place, gradient, left)


def right_kernel(place, *refs):
    pieces, rights = refs[:REP], refs[REP : REP + 7]
    out, total, full, wide_rows = refs[REP + 7 :]
    height, size = full.shape
    width = size // REP
    halves, _, half = wide_rows.shape
    rows = out.shape[2]
    part = rows // REP
    for k, piece in enumerate(pieces):
        at = pl.multiple_of(lax.rem(place[0] + (REP - k), REP) * width, width)
        full[:, pl.ds(at, width)] = piece[0]
    squares = jnp.zeros((8, width), jnp.float32)
    middle = size // 2
    for k in range(REP):
        if k == 0:
            product = jnp.dot(full[...], rights[0][0], preferred_element_type=jnp.float32)
        else:
            top, bottom = rights[2 * k - 1], rights[2 * k]
            product = jnp.dot(full[:, :middle], top[0], preferred_element_type=jnp.float32)
            product = product + jnp.dot(
                full[:, middle:], bottom[0], preferred_element_type=jnp.float32
            )
        squares = squares + jnp.sum((product * product).reshape(height // 8, 8, width), axis=0)
        for j in range(part):
            for h in range(halves):
                wide_rows[h, pl.ds(k * part + j, OWNERS, stride=rows), :] = product[
                    j * OWNERS : (j + 1) * OWNERS, h * half : (h + 1) * half
                ]
    for h in range(halves):
        low = wide_rows[h].astype(jnp.bfloat16).reshape(OWNERS, rows, half)
        out[:, 0, :, h * half : (h + 1) * half] = low
    total[0] = jnp.sum(squares, axis=0, keepdims=True)


def right_multiply(place, pieces, rights):
    count, height, width = pieces[0].shape
    size = rights[0].shape[1]
    rows = size // OWNERS
    return pl.pallas_call(
        right_kernel,
        grid=(count,),
        out_shape=[
            jax.ShapeDtypeStruct((OWNERS, count, rows, width), jnp.bfloat16),
            jax.ShapeDtypeStruct((count, 1, width), jnp.float32),
        ],
        in_specs=[SMEM]
        + [pl.BlockSpec((1, height, width), lambda i: (i, 0, 0))] * 4
        + [pl.BlockSpec((1,) + r.shape[1:], lambda i: (i, 0, 0)) for r in rights],
        out_specs=[
            pl.BlockSpec((OWNERS, 1, rows, width), lambda i: (0, i, 0, 0)),
            pl.BlockSpec((1, 1, width), lambda i: (i, 0, 0)),
        ],
        scratch_shapes=[
            pltpu.VMEM((height, size), jnp.bfloat16),
            pltpu.VMEM((width // 128, size, 128), jnp.float32),
        ],
        compiler_params=pltpu.CompilerParams(vmem_limit_bytes=ROOM),
        cost_estimate=pl.CostEstimate(
            flops=count * 2 * size * size * width,
            bytes_accessed=count * 4 * size * size,
            transcendentals=0,
        ),
        name="right_multiply",
    )(place, *pieces, *rights)


def split_kernel(owner, slot, back01, back2, out, held):
    _, groups, rows, _ = out.shape
    part = rows // REP

    held[:, :2] = back01[...]
    held[:, 2] = back2[:, 0]

    @pl.loop(0, groups)
    def _(g):
        parts = []
        for i in range(REP):
            b = g * REP + i
            parts.append(wide(held[owner[b], slot[b]]))
        for k in range(REP):
            joined = [p[k * part : (k + 1) * part] for p in parts]
            out[(REP - k) % REP, g] = jnp.concatenate(joined, axis=0).astype(jnp.bfloat16)


def split_blocks(owner, slot, back01, back2):
    blocks = owner.shape[0]
    _, _, rows, width = back01.shape
    return pl.pallas_call(
        split_kernel,
        out_shape=jax.ShapeDtypeStruct((REP, blocks // REP, rows, width), jnp.bfloat16),
        in_specs=[SMEM] * 2 + [VMEM] * 2,
        out_specs=VMEM,
        scratch_shapes=[pltpu.VMEM((OWNERS, CAP, rows, width), jnp.bfloat16)],
        compiler_params=pltpu.CompilerParams(vmem_limit_bytes=ROOM),
        name="split_blocks",
    )(owner, slot, back01, back2)


def join_kernel(place, ratio, own, first, second, third, out, held):
    groups, rows, _ = own.shape
    part = rows // REP
    for k, piece in enumerate((own, first, second, third)):
        held[lax.rem(place[0] + (REP - k), REP)] = piece[...]

    @pl.loop(0, groups)
    def _(g):
        parts = [wide(held[q, g]) for q in range(REP)]
        for i in range(REP):
            joined = [p[i * part : (i + 1) * part] for p in parts]
            out[g * REP + i] = jnp.concatenate(joined, axis=0) * ratio[g * REP + i]


def join_blocks(place, ratio, pieces):
    groups, rows, width = pieces[0].shape
    return pl.pallas_call(
        join_kernel,
        out_shape=jax.ShapeDtypeStruct((groups * REP, rows, width), jnp.float32),
        in_specs=[SMEM] * 2 + [VMEM] * 4,
        out_specs=VMEM,
        scratch_shapes=[pltpu.VMEM((REP, groups, rows, width), jnp.bfloat16)],
        compiler_params=pltpu.CompilerParams(vmem_limit_bytes=ROOM),
        name="join_blocks",
    )(place, ratio, *pieces)


def adam_squares(low, moment):
    gradient = wide(low)
    second = second_decay * moment + (1.0 - second_decay) * gradient * gradient
    direction = gradient / (jnp.sqrt(second) + adam_epsilon)
    return jnp.sum(direction * direction, axis=(1, 2))


def exchange(value):
    return lax.all_to_all(value, "fsdp", split_axis=0, concat_axis=0)


def after(value, *others):
    return lax.optimization_barrier((value, *others))[0]


def shards(grad_parts, moment, owner, left_root, right_root):
    place = lax.axis_index("rep")
    place_ref = place.astype(jnp.int32).reshape(1)
    blocks, rows, columns = moment.shape
    slot = block_slots(owner)
    numbers = jnp.arange(blocks, dtype=jnp.int32)
    target = slot * OWNERS + owner
    places = jnp.arange(OWNERS * CAP, dtype=jnp.int32)
    matched = places[:, None] == target[None, :]
    source = jnp.sum(jnp.where(matched, numbers[None, :], 0), axis=1)
    gradient = grad_parts[0]
    pieces = [
        lax.dynamic_slice(
            gradient, (0, 0, lax.rem(place + k, REP) * columns), (blocks, rows, columns)
        )
        for k in range(REP)
    ]
    terms, passing = sum_over_rep(pieces)
    rights01 = gather_over_rep(right_root[0, :2], *passing)
    low, packed01, packed2 = sum_pack(source, terms)
    owned01 = exchange(packed01)
    owned2 = exchange(after(packed2, owned01))
    adam = lax.psum(adam_squares(low, moment), "rep")

    def spread(sent):
        return [sent[0]] + [shift(sent[k], k) for k in (1, 2, 3)]

    sent01 = left_multiply(after(place_ref, *near(rights01)), owned01, left_root[0], 0)
    held01 = spread(sent01)
    rights2 = gather_over_rep(right_root[0, 2:], *held01)
    sent2 = left_multiply(after(place_ref, sent01), owned2, left_root[0], 2)
    result01, square01 = right_multiply(after(place_ref, sent2), held01, rights01)
    back01 = exchange(result01)
    held2 = spread(sent2)
    result2, square2 = right_multiply(after(place_ref, result01), held2, rights2)
    back2 = exchange(after(result2, back01))
    squares = lax.psum(jnp.sum(jnp.concatenate([square01, square2]), axis=(1, 2)), "rep")
    known = jnp.concatenate([adam, squares, jnp.zeros((128 - blocks - CAP,), jnp.float32)])
    known = jnp.broadcast_to(known[None, None, :], (OWNERS, 1, 128))
    sent = split_blocks(owner, slot, back01, back2)
    known = exchange(after(known, back2))[:, 0]
    adam_norm = jnp.sqrt(jnp.sum(known[:, :blocks], axis=0))
    by_place = jnp.transpose(known[:, blocks : blocks + CAP]).reshape(OWNERS * CAP, 1)
    shampoo_norm = jnp.sqrt(jnp.sum(jnp.where(matched, by_place, 0.0), axis=0))
    ratio = adam_norm / (shampoo_norm + norm_epsilon)
    held = spread(sent)
    return join_blocks(place_ref, ratio, held)


def solution(mesh):
    in_specs = (
        P("rep", None, "fsdp", None),
        P(None, "fsdp", "rep"),
        P(),
        P("fsdp", None, None, None),
        P("fsdp", None, None, "rep"),
    )
    out_specs = P(None, "fsdp", "rep")
    return jax.shard_map(shards, mesh=mesh, in_specs=in_specs, out_specs=out_specs, check_vma=False)
```

```python
import jax
import jax.numpy as jnp
from jax import lax
from jax.experimental import pallas as pl
from jax.experimental.pallas import tpu as pltpu
from jax.sharding import PartitionSpec as P

second_decay = 0.99
adam_epsilon = 1e-08
norm_epsilon = 1e-06

REP = 4
OWNERS = 64
CAP = 3
VMEM = pl.BlockSpec(memory_space=pltpu.VMEM)
SMEM = pl.BlockSpec(memory_space=pltpu.SMEM)
ROOM = 48 * 1024 * 1024


def block_slots(owner):
    count = owner.shape[0]
    numbers = jnp.arange(count, dtype=jnp.int32)
    same = owner[:, None] == owner[None, :]
    earlier = numbers[None, :] < numbers[:, None]
    return jnp.sum(jnp.where(same & earlier, 1, 0), axis=1).astype(jnp.int32)


def shift(value, step):
    return lax.ppermute(value, "rep", [(i, (i + step) % REP) for i in range(REP)])


def wide(value):
    return value.astype(jnp.float32)


def sum_over_rep(pieces):
    middle = pieces[0].shape[0] // 2
    top, bottom = slice(0, middle), slice(middle, None)
    far_right = shift(pieces[2][top], 1)
    far_left = shift(pieces[2][bottom], 3)
    near_right = shift(pieces[1][bottom], 1)
    near_left = shift(pieces[3][top], 3)
    on_right = (wide(pieces[1][top]) + wide(far_right)).astype(jnp.bfloat16)
    on_left = (wide(pieces[3][bottom]) + wide(far_left)).astype(jnp.bfloat16)
    last_right = shift(on_right, 1)
    last_left = shift(on_left, 3)
    return (pieces[0], near_left, last_right, near_right, last_left), (on_right, on_left)


def gather_over_rep(value, *others):
    middle = value.shape[1] // 2
    top, bottom = after((value[:, :middle], value[:, middle:]), *others)
    left_top = shift(top, 1)
    right_bottom = shift(bottom, 3)
    left_bottom = shift(bottom, 1)
    right_top = shift(top, 3)
    far_top = shift(left_top, 1)
    far_bottom = shift(right_bottom, 3)
    return value, left_top, left_bottom, far_top, far_bottom, right_top, right_bottom


def sum_pack_kernel(source, own, near_left, last_right, near_right, last_left, low, out):
    middle = near_left.shape[0]

    @pl.loop(0, middle)
    def _(b):
        low[b] = (wide(own[b]) + (wide(near_left[b]) + wide(last_right[b]))).astype(jnp.bfloat16)
        c = middle + b
        low[c] = (wide(own[c]) + (wide(near_right[b]) + wide(last_left[b]))).astype(jnp.bfloat16)

    @pl.loop(0, OWNERS)
    def _(o):
        for s in range(CAP):
            out[o, s] = low[source[s * OWNERS + o]]


def sum_pack(source, terms):
    blocks, rows, columns = terms[0].shape
    return pl.pallas_call(
        sum_pack_kernel,
        out_shape=[
            jax.ShapeDtypeStruct((blocks, rows, columns), jnp.bfloat16),
            jax.ShapeDtypeStruct((OWNERS, CAP, rows, columns), jnp.bfloat16),
        ],
        in_specs=[SMEM] + [VMEM] * 5,
        out_specs=[VMEM, VMEM],
        compiler_params=pltpu.CompilerParams(vmem_limit_bytes=ROOM),
        name="sum_pack",
    )(source, *terms)


def left_kernel(first, place, gradient, left, out, wide_rows):
    halves, size, half = wide_rows.shape
    width = halves * half
    rows = gradient.shape[2]
    part = rows // REP
    s = pl.program_id(0)
    low = gradient[:, first + s].reshape(size, width)
    tile = size // 4
    for i in range(4):
        at = slice(i * tile, (i + 1) * tile)
        product = jnp.dot(left[0, at, :], low, preferred_element_type=jnp.float32)
        for h in range(halves):
            wide_rows[h, at, :] = product[:, h * half : (h + 1) * half]
    for target in range(REP):
        k = lax.rem(target + REP - place[0], REP)
        for j in range(part):
            for h in range(halves):
                strided = wide_rows[h, pl.ds(target * part + j, OWNERS, stride=rows), :]
                at = slice(j * OWNERS, (j + 1) * OWNERS), slice(h * half, (h + 1) * half)
                out[(k, 0) + at] = strided.astype(jnp.bfloat16)


def left_multiply(place, gradient, left, first, count):
    size, width = left.shape[1], gradient.shape[3]
    return pl.pallas_call(
        lambda *refs: left_kernel(first, *refs),
        grid=(count,),
        out_shape=jax.ShapeDtypeStruct((REP, count, size // REP, width), jnp.bfloat16),
        in_specs=[SMEM, VMEM, pl.BlockSpec((1, size, size), lambda i: (first + i, 0, 0))],
        out_specs=pl.BlockSpec((REP, 1, size // REP, width), lambda i: (0, i, 0, 0)),
        scratch_shapes=[pltpu.VMEM((width // 128, size, 128), jnp.float32)],
        compiler_params=pltpu.CompilerParams(vmem_limit_bytes=ROOM),
        cost_estimate=pl.CostEstimate(
            flops=count * 2 * size * size * width,
            bytes_accessed=count * 4 * size * size,
            transcendentals=0,
        ),
        name="left_multiply",
    )(place, gradient, left)


def right_kernel(place, *refs):
    pieces, rights = refs[:REP], refs[REP : REP + 7]
    out, total, full, wide_rows = refs[-4:]
    height, size = full.shape
    width = size // REP
    halves, _, half = wide_rows.shape
    rows = out.shape[2]
    part = rows // REP
    for k, piece in enumerate(pieces):
        at = pl.multiple_of(lax.rem(place[0] + (REP - k), REP) * width, width)
        full[:, pl.ds(at, width)] = piece[0]
    squares = jnp.zeros((8, width), jnp.float32)
    middle = size // 2
    for k in range(REP):
        if k == 0:
            product = jnp.dot(full[...], rights[0][0], preferred_element_type=jnp.float32)
        else:
            top, bottom = rights[2 * k - 1], rights[2 * k]
            product = jnp.dot(full[:, :middle], top[0], preferred_element_type=jnp.float32)
            product = product + jnp.dot(
                full[:, middle:], bottom[0], preferred_element_type=jnp.float32
            )
        squares = squares + jnp.sum((product * product).reshape(height // 8, 8, width), axis=0)
        for j in range(part):
            for h in range(halves):
                wide_rows[h, pl.ds(k * part + j, OWNERS, stride=rows), :] = product[
                    j * OWNERS : (j + 1) * OWNERS, h * half : (h + 1) * half
                ]
    for h in range(halves):
        low = wide_rows[h].astype(jnp.bfloat16).reshape(OWNERS, rows, half)
        out[:, 0, :, h * half : (h + 1) * half] = low
    total[0] = jnp.sum(squares, axis=0, keepdims=True)


def right_multiply(place, pieces, rights, first, before):
    slots, height, width = pieces[0].shape
    count, size = rights[0].shape[:2]
    rows = size // OWNERS
    kept = [] if before is None else [before]
    return pl.pallas_call(
        right_kernel,
        grid=(count,),
        out_shape=[
            jax.ShapeDtypeStruct((OWNERS, slots, rows, width), jnp.bfloat16),
            jax.ShapeDtypeStruct((count, 1, width), jnp.float32),
        ],
        in_specs=[SMEM]
        + [pl.BlockSpec((1, height, width), lambda i: (first + i, 0, 0))] * 4
        + [pl.BlockSpec((1,) + r.shape[1:], lambda i: (i, 0, 0)) for r in rights]
        + [pl.BlockSpec(memory_space=pl.ANY) for _ in kept],
        out_specs=[
            pl.BlockSpec((OWNERS, 1, rows, width), lambda i: (0, first + i, 0, 0)),
            pl.BlockSpec((1, 1, width), lambda i: (i, 0, 0)),
        ],
        scratch_shapes=[
            pltpu.VMEM((height, size), jnp.bfloat16),
            pltpu.VMEM((width // 128, size, 128), jnp.float32),
        ],
        input_output_aliases={1 + len(pieces) + len(rights): 0} if kept else {},
        compiler_params=pltpu.CompilerParams(vmem_limit_bytes=ROOM),
        cost_estimate=pl.CostEstimate(
            flops=count * 2 * size * size * width,
            bytes_accessed=count * 4 * size * size,
            transcendentals=0,
        ),
        name="right_multiply",
    )(place, *pieces, *rights, *kept)


def split_kernel(owner, slot, back, out):
    _, groups, rows, _ = out.shape
    part = rows // REP

    @pl.loop(0, groups)
    def _(g):
        parts = []
        for i in range(REP):
            b = g * REP + i
            parts.append(wide(back[owner[b], slot[b]]))
        for k in range(REP):
            joined = [p[k * part : (k + 1) * part] for p in parts]
            out[(REP - k) % REP, g] = jnp.concatenate(joined, axis=0).astype(jnp.bfloat16)


def split_blocks(owner, slot, back):
    blocks = owner.shape[0]
    _, _, rows, width = back.shape
    return pl.pallas_call(
        split_kernel,
        out_shape=jax.ShapeDtypeStruct((REP, blocks // REP, rows, width), jnp.bfloat16),
        in_specs=[SMEM] * 2 + [VMEM],
        out_specs=VMEM,
        compiler_params=pltpu.CompilerParams(vmem_limit_bytes=ROOM),
        name="split_blocks",
    )(owner, slot, back)


def join_kernel(place, ratio, own, first, second, third, out, held):
    groups, rows, _ = own.shape
    part = rows // REP
    for k, piece in enumerate((own, first, second, third)):
        held[lax.rem(place[0] + (REP - k), REP)] = piece[...]

    @pl.loop(0, groups)
    def _(g):
        parts = [wide(held[q, g]) for q in range(REP)]
        for i in range(REP):
            joined = [p[i * part : (i + 1) * part] for p in parts]
            out[g * REP + i] = jnp.concatenate(joined, axis=0) * ratio[g * REP + i]


def join_blocks(place, ratio, pieces):
    groups, rows, width = pieces[0].shape
    return pl.pallas_call(
        join_kernel,
        out_shape=jax.ShapeDtypeStruct((groups * REP, rows, width), jnp.float32),
        in_specs=[SMEM] * 2 + [VMEM] * 4,
        out_specs=VMEM,
        scratch_shapes=[pltpu.VMEM((REP, groups, rows, width), jnp.bfloat16)],
        compiler_params=pltpu.CompilerParams(vmem_limit_bytes=ROOM),
        name="join_blocks",
    )(place, ratio, *pieces)


def adam_squares(low, moment):
    gradient = wide(low)
    second = second_decay * moment + (1.0 - second_decay) * gradient * gradient
    direction = gradient / (jnp.sqrt(second) + adam_epsilon)
    return jnp.sum(direction * direction, axis=(1, 2))


def exchange(value):
    return lax.all_to_all(value, "fsdp", split_axis=0, concat_axis=0)


def after(value, *others):
    return lax.optimization_barrier((value, *others))[0]


def shards(grad_parts, moment, owner, left_root, right_root):
    place = lax.axis_index("rep")
    place_ref = place.astype(jnp.int32).reshape(1)
    blocks, rows, columns = moment.shape
    slot = block_slots(owner)
    numbers = jnp.arange(blocks, dtype=jnp.int32)
    target = slot * OWNERS + owner
    places = jnp.arange(OWNERS * CAP, dtype=jnp.int32)
    matched = places[:, None] == target[None, :]
    source = jnp.sum(jnp.where(matched, numbers[None, :], 0), axis=1)
    gradient = grad_parts[0]
    pieces = [
        lax.dynamic_slice(
            gradient, (0, 0, lax.rem(place + k, REP) * columns), (blocks, rows, columns)
        )
        for k in range(REP)
    ]
    terms, passing = sum_over_rep(pieces)
    rights01 = gather_over_rep(right_root[0, :2], *passing)
    rights2 = gather_over_rep(right_root[0, 2:], *rights01)
    low, packed = sum_pack(source, terms)
    owned = exchange(packed)
    adam = lax.psum(adam_squares(low, moment), "rep")

    def spread(sent):
        return [sent[0]] + [shift(sent[k], k) for k in (1, 2, 3)]

    sent = left_multiply(after(place_ref, *rights01), owned, left_root[0], 0, CAP)
    held = spread(sent)
    result, square01 = right_multiply(place_ref, held, rights01, 0, None)
    result, square2 = right_multiply(place_ref, held, rights2, 2, result)
    back = exchange(result)
    squares = lax.psum(jnp.sum(jnp.concatenate([square01, square2]), axis=(1, 2)), "rep")
    known = jnp.concatenate([adam, squares, jnp.zeros((128 - blocks - CAP,), jnp.float32)])
    known = jnp.broadcast_to(known[None, None, :], (OWNERS, 1, 128))
    sent = split_blocks(owner, slot, back)
    known = exchange(after(known, back))[:, 0]
    adam_norm = jnp.sqrt(jnp.sum(known[:, :blocks], axis=0))
    by_place = jnp.transpose(known[:, blocks : blocks + CAP]).reshape(OWNERS * CAP, 1)
    shampoo_norm = jnp.sqrt(jnp.sum(jnp.where(matched, by_place, 0.0), axis=0))
    ratio = adam_norm / (shampoo_norm + norm_epsilon)
    held = spread(sent)
    return join_blocks(place_ref, ratio, held)


def solution(mesh):
    in_specs = (
        P("rep", None, "fsdp", None),
        P(None, "fsdp", "rep"),
        P(),
        P("fsdp", None, None, None),
        P("fsdp", None, None, "rep"),
    )
    out_specs = P(None, "fsdp", "rep")
    return jax.shard_map(shards, mesh=mesh, in_specs=in_specs, out_specs=out_specs, check_vma=False)
```

```python
import jax
import jax.numpy as jnp
from jax import lax
from jax.experimental import pallas as pl
from jax.experimental.pallas import tpu as pltpu
from jax.sharding import PartitionSpec as P

second_decay = 0.99
adam_epsilon = 1e-08
norm_epsilon = 1e-06

REP = 4
OWNERS = 64
CAP = 3
VMEM = pl.BlockSpec(memory_space=pltpu.VMEM)
SMEM = pl.BlockSpec(memory_space=pltpu.SMEM)
ROOM = 48 * 1024 * 1024


def block_slots(owner):
    count = owner.shape[0]
    numbers = jnp.arange(count, dtype=jnp.int32)
    same = owner[:, None] == owner[None, :]
    earlier = numbers[None, :] < numbers[:, None]
    return jnp.sum(jnp.where(same & earlier, 1, 0), axis=1).astype(jnp.int32)


def shift(value, step):
    return lax.ppermute(value, "rep", [(i, (i + step) % REP) for i in range(REP)])


def wide(value):
    return value.astype(jnp.float32)


def sum_over_rep(pieces):
    middle = pieces[0].shape[0] // 2
    top, bottom = slice(0, middle), slice(middle, None)
    far_right = shift(pieces[2][top], 1)
    far_left = shift(pieces[2][bottom], 3)
    near_right = shift(pieces[1][bottom], 1)
    near_left = shift(pieces[3][top], 3)
    on_right = (wide(pieces[1][top]) + wide(far_right)).astype(jnp.bfloat16)
    on_left = (wide(pieces[3][bottom]) + wide(far_left)).astype(jnp.bfloat16)
    last_right = shift(on_right, 1)
    last_left = shift(on_left, 3)
    return (pieces[0], near_left, last_right, near_right, last_left), (on_right, on_left)


def gather_over_rep(value, *others):
    middle = value.shape[1] // 2
    top, bottom = after((value[:, :middle], value[:, middle:]), *others)
    left_top = shift(top, 1)
    right_bottom = shift(bottom, 3)
    left_bottom = shift(bottom, 1)
    right_top = shift(top, 3)
    far_top = shift(left_top, 1)
    far_bottom = shift(right_bottom, 3)
    return value, left_top, left_bottom, far_top, far_bottom, right_top, right_bottom


def sum_pack_kernel(source, own, near_left, last_right, near_right, last_left, low, out):
    middle = near_left.shape[0]

    @pl.loop(0, middle, unroll=4)
    def _(b):
        low[b] = (wide(own[b]) + (wide(near_left[b]) + wide(last_right[b]))).astype(jnp.bfloat16)
        c = middle + b
        low[c] = (wide(own[c]) + (wide(near_right[b]) + wide(last_left[b]))).astype(jnp.bfloat16)

    @pl.loop(0, OWNERS, unroll=4)
    def _(o):
        for s in range(CAP):
            out[o, s] = low[source[s * OWNERS + o]]


def sum_pack(source, terms):
    blocks, rows, columns = terms[0].shape
    return pl.pallas_call(
        sum_pack_kernel,
        out_shape=[
            jax.ShapeDtypeStruct((blocks, rows, columns), jnp.bfloat16),
            jax.ShapeDtypeStruct((OWNERS, CAP, rows, columns), jnp.bfloat16),
        ],
        in_specs=[SMEM] + [VMEM] * 5,
        out_specs=[VMEM, VMEM],
        compiler_params=pltpu.CompilerParams(vmem_limit_bytes=ROOM),
        name="sum_pack",
    )(source, *terms)


def left_kernel(first, place, gradient, left, out, wide_rows):
    halves, size, half = wide_rows.shape
    width = halves * half
    rows = gradient.shape[2]
    part = rows // REP
    s = pl.program_id(0)
    low = gradient[:, first + s].reshape(size, width)
    tile = size // 4
    for i in range(4):
        at = slice(i * tile, (i + 1) * tile)
        product = jnp.dot(left[0, at, :], low, preferred_element_type=jnp.float32)
        for h in range(halves):
            wide_rows[h, at, :] = product[:, h * half : (h + 1) * half]
    for target in range(REP):
        k = lax.rem(target + REP - place[0], REP)
        for j in range(part):
            for h in range(halves):
                strided = wide_rows[h, pl.ds(target * part + j, OWNERS, stride=rows), :]
                at = slice(j * OWNERS, (j + 1) * OWNERS), slice(h * half, (h + 1) * half)
                out[(k, 0) + at] = strided.astype(jnp.bfloat16)


def left_multiply(place, gradient, left, first, count):
    size, width = left.shape[1], gradient.shape[3]
    return pl.pallas_call(
        lambda *refs: left_kernel(first, *refs),
        grid=(count,),
        out_shape=jax.ShapeDtypeStruct((REP, count, size // REP, width), jnp.bfloat16),
        in_specs=[SMEM, VMEM, pl.BlockSpec((1, size, size), lambda i: (first + i, 0, 0))],
        out_specs=pl.BlockSpec((REP, 1, size // REP, width), lambda i: (0, i, 0, 0)),
        scratch_shapes=[pltpu.VMEM((width // 128, size, 128), jnp.float32)],
        compiler_params=pltpu.CompilerParams(vmem_limit_bytes=ROOM),
        cost_estimate=pl.CostEstimate(
            flops=count * 2 * size * size * width,
            bytes_accessed=count * 4 * size * size,
            transcendentals=0,
        ),
        name="left_multiply",
    )(place, gradient, left)


def right_kernel(place, *refs):
    pieces, rights = refs[:REP], refs[REP : REP + 7]
    out, total, full, wide_rows = refs[REP + 7 :]
    height, size = full.shape
    width = size // REP
    halves, _, half = wide_rows.shape
    rows = out.shape[2]
    part = rows // REP
    for k, piece in enumerate(pieces):
        at = pl.multiple_of(lax.rem(place[0] + (REP - k), REP) * width, width)
        full[:, pl.ds(at, width)] = piece[0]
    squares = jnp.zeros((8, width), jnp.float32)
    middle = size // 2
    for k in range(REP):
        if k == 0:
            product = jnp.dot(full[...], rights[0][0], preferred_element_type=jnp.float32)
        else:
            top, bottom = rights[2 * k - 1], rights[2 * k]
            product = jnp.dot(full[:, :middle], top[0], preferred_element_type=jnp.float32)
            product = product + jnp.dot(
                full[:, middle:], bottom[0], preferred_element_type=jnp.float32
            )
        squares = squares + jnp.sum((product * product).reshape(height // 8, 8, width), axis=0)
        for j in range(part):
            for h in range(halves):
                wide_rows[h, pl.ds(k * part + j, OWNERS, stride=rows), :] = product[
                    j * OWNERS : (j + 1) * OWNERS, h * half : (h + 1) * half
                ]
    for h in range(halves):
        low = wide_rows[h].astype(jnp.bfloat16).reshape(OWNERS, rows, half)
        out[:, 0, :, h * half : (h + 1) * half] = low
    total[0] = jnp.sum(squares, axis=0, keepdims=True)


def right_multiply(place, pieces, rights):
    count, height, width = pieces[0].shape
    size = rights[0].shape[1]
    rows = size // OWNERS
    return pl.pallas_call(
        right_kernel,
        grid=(count,),
        out_shape=[
            jax.ShapeDtypeStruct((OWNERS, count, rows, width), jnp.bfloat16),
            jax.ShapeDtypeStruct((count, 1, width), jnp.float32),
        ],
        in_specs=[SMEM]
        + [pl.BlockSpec((1, height, width), lambda i: (i, 0, 0))] * 4
        + [pl.BlockSpec((1,) + r.shape[1:], lambda i: (i, 0, 0)) for r in rights],
        out_specs=[
            pl.BlockSpec((OWNERS, 1, rows, width), lambda i: (0, i, 0, 0)),
            pl.BlockSpec((1, 1, width), lambda i: (i, 0, 0)),
        ],
        scratch_shapes=[
            pltpu.VMEM((height, size), jnp.bfloat16),
            pltpu.VMEM((width // 128, size, 128), jnp.float32),
        ],
        compiler_params=pltpu.CompilerParams(vmem_limit_bytes=ROOM),
        cost_estimate=pl.CostEstimate(
            flops=count * 2 * size * size * width,
            bytes_accessed=count * 4 * size * size,
            transcendentals=0,
        ),
        name="right_multiply",
    )(place, *pieces, *rights)


def split_kernel(owner, slot, back01, back2, out, held):
    _, groups, rows, _ = out.shape
    part = rows // REP

    held[:, :2] = back01[...]
    held[:, 2] = back2[:, 0]

    @pl.loop(0, groups, unroll=2)
    def _(g):
        parts = []
        for i in range(REP):
            b = g * REP + i
            parts.append(wide(held[owner[b], slot[b]]))
        for k in range(REP):
            joined = [p[k * part : (k + 1) * part] for p in parts]
            out[(REP - k) % REP, g] = jnp.concatenate(joined, axis=0).astype(jnp.bfloat16)


def split_blocks(owner, slot, back01, back2):
    blocks = owner.shape[0]
    _, _, rows, width = back01.shape
    return pl.pallas_call(
        split_kernel,
        out_shape=jax.ShapeDtypeStruct((REP, blocks // REP, rows, width), jnp.bfloat16),
        in_specs=[SMEM] * 2 + [VMEM] * 2,
        out_specs=VMEM,
        scratch_shapes=[pltpu.VMEM((OWNERS, CAP, rows, width), jnp.bfloat16)],
        compiler_params=pltpu.CompilerParams(vmem_limit_bytes=ROOM),
        name="split_blocks",
    )(owner, slot, back01, back2)


def join_kernel(place, ratio, own, first, second, third, out, held):
    groups, rows, _ = own.shape
    part = rows // REP
    for k, piece in enumerate((own, first, second, third)):
        held[lax.rem(place[0] + (REP - k), REP)] = piece[...]

    @pl.loop(0, groups, unroll=2)
    def _(g):
        parts = [wide(held[q, g]) for q in range(REP)]
        for i in range(REP):
            joined = [p[i * part : (i + 1) * part] for p in parts]
            out[g * REP + i] = jnp.concatenate(joined, axis=0) * ratio[g * REP + i]


def join_blocks(place, ratio, pieces):
    groups, rows, width = pieces[0].shape
    return pl.pallas_call(
        join_kernel,
        out_shape=jax.ShapeDtypeStruct((groups * REP, rows, width), jnp.float32),
        in_specs=[SMEM] * 2 + [VMEM] * 4,
        out_specs=VMEM,
        scratch_shapes=[pltpu.VMEM((REP, groups, rows, width), jnp.bfloat16)],
        compiler_params=pltpu.CompilerParams(vmem_limit_bytes=ROOM),
        name="join_blocks",
    )(place, ratio, *pieces)


def adam_squares(low, moment):
    gradient = wide(low)
    second = second_decay * moment + (1.0 - second_decay) * gradient * gradient
    direction = gradient / (jnp.sqrt(second) + adam_epsilon)
    return jnp.sum(direction * direction, axis=(1, 2))


def exchange(value):
    return lax.all_to_all(value, "fsdp", split_axis=0, concat_axis=0)


def after(value, *others):
    return lax.optimization_barrier((value, *others))[0]


def shards(grad_parts, moment, owner, left_root, right_root):
    place = lax.axis_index("rep")
    place_ref = place.astype(jnp.int32).reshape(1)
    blocks, rows, columns = moment.shape
    slot = block_slots(owner)
    numbers = jnp.arange(blocks, dtype=jnp.int32)
    target = slot * OWNERS + owner
    places = jnp.arange(OWNERS * CAP, dtype=jnp.int32)
    matched = places[:, None] == target[None, :]
    source = jnp.sum(jnp.where(matched, numbers[None, :], 0), axis=1)
    gradient = grad_parts[0]
    pieces = [
        lax.dynamic_slice(
            gradient, (0, 0, lax.rem(place + k, REP) * columns), (blocks, rows, columns)
        )
        for k in range(REP)
    ]
    terms, passing = sum_over_rep(pieces)
    rights01 = gather_over_rep(right_root[0, :2], *passing)
    low, packed = sum_pack(source, terms)
    owned = exchange(packed)
    adam = lax.psum(adam_squares(low, moment), "rep")

    def spread(sent):
        return [sent[0]] + [shift(sent[k], k) for k in (1, 2, 3)]

    sent01 = left_multiply(after(place_ref, *rights01), owned, left_root[0], 0, 2)
    across = shift(sent01[2][:1], 2)
    back_once = shift(sent01[2][1:], 3)
    held01 = [sent01[0], shift(sent01[1], 1), None, shift(sent01[3], 3)]
    held01[2] = jnp.concatenate([across, shift(back_once, 3)])
    result01, square01 = right_multiply(place_ref, held01, rights01)
    back01 = exchange(result01)
    rights2 = gather_over_rep(right_root[0, 2:], *held01)
    sent2 = left_multiply(after(place_ref, *held01), owned, left_root[0], 2, 1)
    held2 = spread(sent2)
    result2, square2 = right_multiply(place_ref, held2, rights2)
    back2 = exchange(after(result2, back01))
    squares = lax.psum(jnp.sum(jnp.concatenate([square01, square2]), axis=(1, 2)), "rep")
    known = jnp.concatenate([adam, squares, jnp.zeros((128 - blocks - CAP,), jnp.float32)])
    known = jnp.broadcast_to(known[None, None, :], (OWNERS, 1, 128))
    sent = split_blocks(owner, slot, back01, back2)
    known = exchange(after(known, sent))[:, 0]
    adam_norm = jnp.sqrt(jnp.sum(known[:, :blocks], axis=0))
    by_place = jnp.transpose(known[:, blocks : blocks + CAP]).reshape(OWNERS * CAP, 1)
    shampoo_norm = jnp.sqrt(jnp.sum(jnp.where(matched, by_place, 0.0), axis=0))
    ratio = adam_norm / (shampoo_norm + norm_epsilon)
    held = spread(sent)
    return join_blocks(place_ref, ratio, held)


def solution(mesh):
    in_specs = (
        P("rep", None, "fsdp", None),
        P(None, "fsdp", "rep"),
        P(),
        P("fsdp", None, None, None),
        P("fsdp", None, None, "rep"),
    )
    out_specs = P(None, "fsdp", "rep")
    return jax.shard_map(shards, mesh=mesh, in_specs=in_specs, out_specs=out_specs, check_vma=False)
```

```python
import jax
import jax.numpy as jnp
from jax import lax
from jax.experimental import pallas as pl
from jax.experimental.pallas import tpu as pltpu
from jax.sharding import PartitionSpec as P

second_decay = 0.99
adam_epsilon = 1e-08
norm_epsilon = 1e-06

REP = 4
OWNERS = 64
CAP = 3
VMEM = pl.BlockSpec(memory_space=pltpu.VMEM)
SMEM = pl.BlockSpec(memory_space=pltpu.SMEM)
ROOM = 48 * 1024 * 1024


def block_slots(owner):
    count = owner.shape[0]
    numbers = jnp.arange(count, dtype=jnp.int32)
    same = owner[:, None] == owner[None, :]
    earlier = numbers[None, :] < numbers[:, None]
    return jnp.sum(jnp.where(same & earlier, 1, 0), axis=1).astype(jnp.int32)


def shift(value, step):
    return lax.ppermute(value, "rep", [(i, (i + step) % REP) for i in range(REP)])


def wide(value):
    return value.astype(jnp.float32)


def sum_over_rep(pieces):
    middle = pieces[0].shape[0] // 2
    top, bottom = slice(0, middle), slice(middle, None)
    far_right = shift(pieces[2][top], 1)
    far_left = shift(pieces[2][bottom], 3)
    near_right = shift(pieces[1][bottom], 1)
    near_left = shift(pieces[3][top], 3)
    on_right = (wide(pieces[1][top]) + wide(far_right)).astype(jnp.bfloat16)
    on_left = (wide(pieces[3][bottom]) + wide(far_left)).astype(jnp.bfloat16)
    last_right = shift(on_right, 1)
    last_left = shift(on_left, 3)
    return (pieces[0], near_left, last_right, near_right, last_left), (on_right, on_left)


def gather_over_rep(value, *others):
    middle = value.shape[1] // 2
    top, bottom = after((value[:, :middle], value[:, middle:]), *others)
    left_top = shift(top, 1)
    right_bottom = shift(bottom, 3)
    left_bottom = shift(bottom, 1)
    right_top = shift(top, 3)
    far_top = shift(left_top, 1)
    far_bottom = shift(right_bottom, 3)
    return value, left_top, left_bottom, far_top, far_bottom, right_top, right_bottom


def sum_pack_kernel(source, own, near_left, last_right, near_right, last_left, low, out):
    middle = near_left.shape[0]

    @pl.loop(0, middle, unroll=4)
    def _(b):
        low[b] = (wide(own[b]) + (wide(near_left[b]) + wide(last_right[b]))).astype(jnp.bfloat16)
        c = middle + b
        low[c] = (wide(own[c]) + (wide(near_right[b]) + wide(last_left[b]))).astype(jnp.bfloat16)

    @pl.loop(0, OWNERS, unroll=4)
    def _(o):
        for s in range(CAP):
            out[o, s] = low[source[s * OWNERS + o]]


def sum_pack(source, terms):
    blocks, rows, columns = terms[0].shape
    return pl.pallas_call(
        sum_pack_kernel,
        out_shape=[
            jax.ShapeDtypeStruct((blocks, rows, columns), jnp.bfloat16),
            jax.ShapeDtypeStruct((OWNERS, CAP, rows, columns), jnp.bfloat16),
        ],
        in_specs=[SMEM] + [VMEM] * 5,
        out_specs=[VMEM, VMEM],
        compiler_params=pltpu.CompilerParams(vmem_limit_bytes=ROOM),
        name="sum_pack",
    )(source, *terms)


def left_kernel(first, place, gradient, left, out, wide_rows):
    halves, size, half = wide_rows.shape
    width = halves * half
    rows = gradient.shape[2]
    part = rows // REP
    s = pl.program_id(0)
    low = gradient[:, first + s].reshape(size, width)
    tile = size // 4
    for i in range(4):
        at = slice(i * tile, (i + 1) * tile)
        product = jnp.dot(left[0, at, :], low, preferred_element_type=jnp.float32)
        for h in range(halves):
            wide_rows[h, at, :] = product[:, h * half : (h + 1) * half]
    for target in range(REP):
        k = lax.rem(target + REP - place[0], REP)
        for j in range(part):
            for h in range(halves):
                strided = wide_rows[h, pl.ds(target * part + j, OWNERS, stride=rows), :]
                at = slice(j * OWNERS, (j + 1) * OWNERS), slice(h * half, (h + 1) * half)
                out[(k, 0) + at] = strided.astype(jnp.bfloat16)


def left_multiply(place, gradient, left, first, count):
    size, width = left.shape[1], gradient.shape[3]
    return pl.pallas_call(
        lambda *refs: left_kernel(first, *refs),
        grid=(count,),
        out_shape=jax.ShapeDtypeStruct((REP, count, size // REP, width), jnp.bfloat16),
        in_specs=[SMEM, VMEM, pl.BlockSpec((1, size, size), lambda i: (first + i, 0, 0))],
        out_specs=pl.BlockSpec((REP, 1, size // REP, width), lambda i: (0, i, 0, 0)),
        scratch_shapes=[pltpu.VMEM((width // 128, size, 128), jnp.float32)],
        compiler_params=pltpu.CompilerParams(vmem_limit_bytes=ROOM),
        cost_estimate=pl.CostEstimate(
            flops=count * 2 * size * size * width,
            bytes_accessed=count * 4 * size * size,
            transcendentals=0,
        ),
        name="left_multiply",
    )(place, gradient, left)


def right_kernel(place, *refs):
    pieces, rights = refs[:REP], refs[REP : REP + 7]
    out, total, full, wide_rows = refs[REP + 7 :]
    height, size = full.shape
    width = size // REP
    halves, _, half = wide_rows.shape
    rows = out.shape[2]
    part = rows // REP
    for k, piece in enumerate(pieces):
        at = pl.multiple_of(lax.rem(place[0] + (REP - k), REP) * width, width)
        full[:, pl.ds(at, width)] = piece[0]
    squares = jnp.zeros((8, width), jnp.float32)
    middle = size // 2
    for k in range(REP):
        if k == 0:
            product = jnp.dot(full[...], rights[0][0], preferred_element_type=jnp.float32)
        else:
            top, bottom = rights[2 * k - 1], rights[2 * k]
            product = jnp.dot(full[:, :middle], top[0], preferred_element_type=jnp.float32)
            product = product + jnp.dot(
                full[:, middle:], bottom[0], preferred_element_type=jnp.float32
            )
        squares = squares + jnp.sum((product * product).reshape(height // 8, 8, width), axis=0)
        for j in range(part):
            for h in range(halves):
                wide_rows[h, pl.ds(k * part + j, OWNERS, stride=rows), :] = product[
                    j * OWNERS : (j + 1) * OWNERS, h * half : (h + 1) * half
                ]
    for h in range(halves):
        low = wide_rows[h].astype(jnp.bfloat16).reshape(OWNERS, rows, half)
        out[:, 0, :, h * half : (h + 1) * half] = low
    total[0] = jnp.sum(squares, axis=0, keepdims=True)


def right_multiply(place, pieces, rights):
    count, height, width = pieces[0].shape
    size = rights[0].shape[1]
    rows = size // OWNERS
    return pl.pallas_call(
        right_kernel,
        grid=(count,),
        out_shape=[
            jax.ShapeDtypeStruct((OWNERS, count, rows, width), jnp.bfloat16),
            jax.ShapeDtypeStruct((count, 1, width), jnp.float32),
        ],
        in_specs=[SMEM]
        + [pl.BlockSpec((1, height, width), lambda i: (i, 0, 0))] * 4
        + [pl.BlockSpec((1,) + r.shape[1:], lambda i: (i, 0, 0)) for r in rights],
        out_specs=[
            pl.BlockSpec((OWNERS, 1, rows, width), lambda i: (0, i, 0, 0)),
            pl.BlockSpec((1, 1, width), lambda i: (i, 0, 0)),
        ],
        scratch_shapes=[
            pltpu.VMEM((height, size), jnp.bfloat16),
            pltpu.VMEM((width // 128, size, 128), jnp.float32),
        ],
        compiler_params=pltpu.CompilerParams(vmem_limit_bytes=ROOM),
        cost_estimate=pl.CostEstimate(
            flops=count * 2 * size * size * width,
            bytes_accessed=count * 4 * size * size,
            transcendentals=0,
        ),
        name="right_multiply",
    )(place, *pieces, *rights)


def split_kernel(owner, slot, back, out):
    _, groups, rows, _ = out.shape
    part = rows // REP

    @pl.loop(0, groups, unroll=2)
    def _(g):
        parts = []
        for i in range(REP):
            b = g * REP + i
            parts.append(wide(back[owner[b], slot[b]]))
        for k in range(REP):
            joined = [p[k * part : (k + 1) * part] for p in parts]
            out[(REP - k) % REP, g] = jnp.concatenate(joined, axis=0).astype(jnp.bfloat16)


def split_blocks(owner, slot, back):
    blocks = owner.shape[0]
    _, _, rows, width = back.shape
    return pl.pallas_call(
        split_kernel,
        out_shape=jax.ShapeDtypeStruct((REP, blocks // REP, rows, width), jnp.bfloat16),
        in_specs=[SMEM] * 2 + [VMEM],
        out_specs=VMEM,
        compiler_params=pltpu.CompilerParams(vmem_limit_bytes=ROOM),
        name="split_blocks",
    )(owner, slot, back)


def join_kernel(place, ratio, own, first, second, third, out, held):
    groups, rows, _ = own.shape
    part = rows // REP
    for k, piece in enumerate((own, first, second, third)):
        held[lax.rem(place[0] + (REP - k), REP)] = piece[...]

    @pl.loop(0, groups, unroll=2)
    def _(g):
        parts = [wide(held[q, g]) for q in range(REP)]
        for i in range(REP):
            joined = [p[i * part : (i + 1) * part] for p in parts]
            out[g * REP + i] = jnp.concatenate(joined, axis=0) * ratio[g * REP + i]


def join_blocks(place, ratio, pieces):
    groups, rows, width = pieces[0].shape
    return pl.pallas_call(
        join_kernel,
        out_shape=jax.ShapeDtypeStruct((groups * REP, rows, width), jnp.float32),
        in_specs=[SMEM] * 2 + [VMEM] * 4,
        out_specs=VMEM,
        scratch_shapes=[pltpu.VMEM((REP, groups, rows, width), jnp.bfloat16)],
        compiler_params=pltpu.CompilerParams(vmem_limit_bytes=ROOM),
        name="join_blocks",
    )(place, ratio, *pieces)


def adam_squares(low, moment):
    gradient = wide(low)
    second = second_decay * moment + (1.0 - second_decay) * gradient * gradient
    direction = gradient / (jnp.sqrt(second) + adam_epsilon)
    return jnp.sum(direction * direction, axis=(1, 2))


def exchange(value):
    return lax.all_to_all(value, "fsdp", split_axis=0, concat_axis=0)


def after(value, *others):
    return lax.optimization_barrier((value, *others))[0]


def shards(grad_parts, moment, owner, left_root, right_root):
    place = lax.axis_index("rep")
    place_ref = place.astype(jnp.int32).reshape(1)
    blocks, rows, columns = moment.shape
    slot = block_slots(owner)
    numbers = jnp.arange(blocks, dtype=jnp.int32)
    target = slot * OWNERS + owner
    places = jnp.arange(OWNERS * CAP, dtype=jnp.int32)
    matched = places[:, None] == target[None, :]
    source = jnp.sum(jnp.where(matched, numbers[None, :], 0), axis=1)
    gradient = grad_parts[0]
    pieces = [
        lax.dynamic_slice(
            gradient, (0, 0, lax.rem(place + k, REP) * columns), (blocks, rows, columns)
        )
        for k in range(REP)
    ]
    terms, passing = sum_over_rep(pieces)
    rights = gather_over_rep(right_root[0], *passing)
    low, packed = sum_pack(source, terms)
    owned = exchange(packed)
    adam = lax.psum(adam_squares(low, moment), "rep")

    def spread(sent):
        return [sent[0]] + [shift(sent[k], k) for k in (1, 2, 3)]

    held = spread(left_multiply(place_ref, owned, left_root[0], 0, CAP))
    result, square = right_multiply(place_ref, held, rights)
    back = exchange(result)
    squares = lax.psum(jnp.sum(square, axis=(1, 2)), "rep")
    known = jnp.concatenate([adam, squares, jnp.zeros((128 - blocks - CAP,), jnp.float32)])
    known = jnp.broadcast_to(known[None, None, :], (OWNERS, 1, 128))
    sent = split_blocks(owner, slot, back)
    known = exchange(after(known, sent))[:, 0]
    adam_norm = jnp.sqrt(jnp.sum(known[:, :blocks], axis=0))
    by_place = jnp.transpose(known[:, blocks : blocks + CAP]).reshape(OWNERS * CAP, 1)
    shampoo_norm = jnp.sqrt(jnp.sum(jnp.where(matched, by_place, 0.0), axis=0))
    ratio = adam_norm / (shampoo_norm + norm_epsilon)
    held = spread(sent)
    return join_blocks(place_ref, ratio, held)


def solution(mesh):
    in_specs = (
        P("rep", None, "fsdp", None),
        P(None, "fsdp", "rep"),
        P(),
        P("fsdp", None, None, None),
        P("fsdp", None, None, "rep"),
    )
    out_specs = P(None, "fsdp", "rep")
    return jax.shard_map(shards, mesh=mesh, in_specs=in_specs, out_specs=out_specs, check_vma=False)
```

```python
import jax
import jax.numpy as jnp
from jax import lax
from jax.experimental import pallas as pl
from jax.experimental.pallas import tpu as pltpu
from jax.sharding import PartitionSpec as P

second_decay = 0.99
adam_epsilon = 1e-08
norm_epsilon = 1e-06

REP = 4
OWNERS = 64
CAP = 3
VMEM = pl.BlockSpec(memory_space=pltpu.VMEM)
SMEM = pl.BlockSpec(memory_space=pltpu.SMEM)
ROOM = 48 * 1024 * 1024


def block_slots(owner):
    count = owner.shape[0]
    numbers = jnp.arange(count, dtype=jnp.int32)
    same = owner[:, None] == owner[None, :]
    earlier = numbers[None, :] < numbers[:, None]
    return jnp.sum(jnp.where(same & earlier, 1, 0), axis=1).astype(jnp.int32)


def shift(value, step):
    return lax.ppermute(value, "rep", [(i, (i + step) % REP) for i in range(REP)])


def wide(value):
    return value.astype(jnp.float32)


def sum_over_rep(pieces):
    middle = pieces[0].shape[0] // 2
    top, bottom = slice(0, middle), slice(middle, None)
    far_right = shift(pieces[2][top], 1)
    far_left = shift(pieces[2][bottom], 3)
    near_right = shift(pieces[1][bottom], 1)
    near_left = shift(pieces[3][top], 3)
    on_right = (wide(pieces[1][top]) + wide(far_right)).astype(jnp.bfloat16)
    on_left = (wide(pieces[3][bottom]) + wide(far_left)).astype(jnp.bfloat16)
    last_right = shift(on_right, 1)
    last_left = shift(on_left, 3)
    return (pieces[0], near_left, last_right, near_right, last_left), (on_right, on_left)


def gather_over_rep(value, *others):
    middle = value.shape[1] // 2
    top, bottom = after((value[:, :middle], value[:, middle:]), *others)
    left_top = shift(top, 1)
    right_bottom = shift(bottom, 3)
    left_bottom = shift(bottom, 1)
    right_top = shift(top, 3)
    far_top = shift(left_top, 1)
    far_bottom = shift(right_bottom, 3)
    return value, left_top, left_bottom, far_top, far_bottom, right_top, right_bottom


def sum_pack_kernel(source, own, near_left, last_right, near_right, last_left, low, out):
    middle = near_left.shape[0]

    @pl.loop(0, middle, unroll=4)
    def _(b):
        low[b] = (wide(own[b]) + (wide(near_left[b]) + wide(last_right[b]))).astype(jnp.bfloat16)
        c = middle + b
        low[c] = (wide(own[c]) + (wide(near_right[b]) + wide(last_left[b]))).astype(jnp.bfloat16)

    @pl.loop(0, OWNERS, unroll=4)
    def _(o):
        for s in range(CAP):
            out[o, s] = low[source[s * OWNERS + o]]


def sum_pack(source, terms):
    blocks, rows, columns = terms[0].shape
    return pl.pallas_call(
        sum_pack_kernel,
        out_shape=[
            jax.ShapeDtypeStruct((blocks, rows, columns), jnp.bfloat16),
            jax.ShapeDtypeStruct((OWNERS, CAP, rows, columns), jnp.bfloat16),
        ],
        in_specs=[SMEM] + [VMEM] * 5,
        out_specs=[VMEM, VMEM],
        compiler_params=pltpu.CompilerParams(vmem_limit_bytes=ROOM),
        name="sum_pack",
    )(source, *terms)


def left_kernel(first, place, gradient, left, out, wide_rows):
    halves, size, half = wide_rows.shape
    width = halves * half
    rows = gradient.shape[2]
    part = rows // REP
    s = pl.program_id(0)
    low = gradient[:, first + s].reshape(size, width)
    tile = size // 4
    for i in range(4):
        at = slice(i * tile, (i + 1) * tile)
        product = jnp.dot(left[0, at, :], low, preferred_element_type=jnp.float32)
        for h in range(halves):
            wide_rows[h, at, :] = product[:, h * half : (h + 1) * half]
    for target in range(REP):
        k = lax.rem(target + REP - place[0], REP)
        for j in range(part):
            for h in range(halves):
                strided = wide_rows[h, pl.ds(target * part + j, OWNERS, stride=rows), :]
                at = slice(j * OWNERS, (j + 1) * OWNERS), slice(h * half, (h + 1) * half)
                out[(k, 0) + at] = strided.astype(jnp.bfloat16)


def left_multiply(place, gradient, left, first, count):
    size, width = left.shape[1], gradient.shape[3]
    return pl.pallas_call(
        lambda *refs: left_kernel(first, *refs),
        grid=(count,),
        out_shape=jax.ShapeDtypeStruct((REP, count, size // REP, width), jnp.bfloat16),
        in_specs=[SMEM, VMEM, pl.BlockSpec((1, size, size), lambda i: (first + i, 0, 0))],
        out_specs=pl.BlockSpec((REP, 1, size // REP, width), lambda i: (0, i, 0, 0)),
        scratch_shapes=[pltpu.VMEM((width // 128, size, 128), jnp.float32)],
        compiler_params=pltpu.CompilerParams(vmem_limit_bytes=ROOM),
        cost_estimate=pl.CostEstimate(
            flops=count * 2 * size * size * width,
            bytes_accessed=count * 4 * size * size,
            transcendentals=0,
        ),
        name="left_multiply",
    )(place, gradient, left)


def right_kernel(place, *refs):
    pieces, rights = refs[: REP + 1], refs[REP + 1 : REP + 8]
    out, total, full, wide_rows = refs[REP + 8 :]
    height, size = full.shape
    width = size // REP
    halves, _, half = wide_rows.shape
    rows = out.shape[2]
    part = rows // REP
    first_row = 0
    for k, piece in zip((0, 1, 2, 2, 3), pieces):
        at = pl.multiple_of(lax.rem(place[0] + (REP - k), REP) * width, width)
        last_row = first_row + piece.shape[1]
        full[first_row:last_row, pl.ds(at, width)] = piece[0]
        first_row = last_row % height
    squares = jnp.zeros((8, width), jnp.float32)
    middle = size // 2
    for k in range(REP):
        if k == 0:
            product = jnp.dot(full[...], rights[0][0], preferred_element_type=jnp.float32)
        else:
            top, bottom = rights[2 * k - 1], rights[2 * k]
            product = jnp.dot(full[:, :middle], top[0], preferred_element_type=jnp.float32)
            product = product + jnp.dot(
                full[:, middle:], bottom[0], preferred_element_type=jnp.float32
            )
        squares = squares + jnp.sum((product * product).reshape(height // 8, 8, width), axis=0)
        for j in range(part):
            for h in range(halves):
                wide_rows[h, pl.ds(k * part + j, OWNERS, stride=rows), :] = product[
                    j * OWNERS : (j + 1) * OWNERS, h * half : (h + 1) * half
                ]
    for h in range(halves):
        low = wide_rows[h].astype(jnp.bfloat16).reshape(OWNERS, rows, half)
        out[:, 0, :, h * half : (h + 1) * half] = low
    total[0] = jnp.sum(squares, axis=0, keepdims=True)


def right_multiply(place, pieces, rights):
    count, height, width = pieces[0].shape
    size = rights[0].shape[1]
    rows = size // OWNERS
    return pl.pallas_call(
        right_kernel,
        grid=(count,),
        out_shape=[
            jax.ShapeDtypeStruct((OWNERS, count, rows, width), jnp.bfloat16),
            jax.ShapeDtypeStruct((count, 1, width), jnp.float32),
        ],
        in_specs=[SMEM]
        + [pl.BlockSpec((1,) + p.shape[1:], lambda i: (i, 0, 0)) for p in pieces]
        + [pl.BlockSpec((1,) + r.shape[1:], lambda i: (i, 0, 0)) for r in rights],
        out_specs=[
            pl.BlockSpec((OWNERS, 1, rows, width), lambda i: (0, i, 0, 0)),
            pl.BlockSpec((1, 1, width), lambda i: (i, 0, 0)),
        ],
        scratch_shapes=[
            pltpu.VMEM((height, size), jnp.bfloat16),
            pltpu.VMEM((width // 128, size, 128), jnp.float32),
        ],
        compiler_params=pltpu.CompilerParams(vmem_limit_bytes=ROOM),
        cost_estimate=pl.CostEstimate(
            flops=count * 2 * size * size * width,
            bytes_accessed=count * 4 * size * size,
            transcendentals=0,
        ),
        name="right_multiply",
    )(place, *pieces, *rights)


def split_kernel(owner, slot, back, out):
    _, groups, rows, _ = out.shape
    part = rows // REP

    @pl.loop(0, groups, unroll=2)
    def _(g):
        parts = []
        for i in range(REP):
            b = g * REP + i
            parts.append(wide(back[owner[b], slot[b]]))
        for k in range(REP):
            joined = [p[k * part : (k + 1) * part] for p in parts]
            out[(REP - k) % REP, g] = jnp.concatenate(joined, axis=0).astype(jnp.bfloat16)


def split_blocks(owner, slot, back):
    blocks = owner.shape[0]
    _, _, rows, width = back.shape
    return pl.pallas_call(
        split_kernel,
        out_shape=jax.ShapeDtypeStruct((REP, blocks // REP, rows, width), jnp.bfloat16),
        in_specs=[SMEM] * 2 + [VMEM],
        out_specs=VMEM,
        compiler_params=pltpu.CompilerParams(vmem_limit_bytes=ROOM),
        name="split_blocks",
    )(owner, slot, back)


def join_kernel(place, ratio, own, first, second, third, out, held):
    groups, rows, _ = own.shape
    part = rows // REP
    for k, piece in enumerate((own, first, second, third)):
        held[lax.rem(place[0] + (REP - k), REP)] = piece[...]

    @pl.loop(0, groups, unroll=2)
    def _(g):
        parts = [wide(held[q, g]) for q in range(REP)]
        for i in range(REP):
            joined = [p[i * part : (i + 1) * part] for p in parts]
            out[g * REP + i] = jnp.concatenate(joined, axis=0) * ratio[g * REP + i]


def join_blocks(place, ratio, pieces):
    groups, rows, width = pieces[0].shape
    return pl.pallas_call(
        join_kernel,
        out_shape=jax.ShapeDtypeStruct((groups * REP, rows, width), jnp.float32),
        in_specs=[SMEM] * 2 + [VMEM] * 4,
        out_specs=VMEM,
        scratch_shapes=[pltpu.VMEM((REP, groups, rows, width), jnp.bfloat16)],
        compiler_params=pltpu.CompilerParams(vmem_limit_bytes=ROOM),
        name="join_blocks",
    )(place, ratio, *pieces)


def adam_squares(low, moment):
    gradient = wide(low)
    second = second_decay * moment + (1.0 - second_decay) * gradient * gradient
    direction = gradient / (jnp.sqrt(second) + adam_epsilon)
    return jnp.sum(direction * direction, axis=(1, 2))


def exchange(value):
    return lax.all_to_all(value, "fsdp", split_axis=0, concat_axis=0)


def after(value, *others):
    return lax.optimization_barrier((value, *others))[0]


def shards(grad_parts, moment, owner, left_root, right_root):
    place = lax.axis_index("rep")
    place_ref = place.astype(jnp.int32).reshape(1)
    blocks, rows, columns = moment.shape
    slot = block_slots(owner)
    numbers = jnp.arange(blocks, dtype=jnp.int32)
    target = slot * OWNERS + owner
    places = jnp.arange(OWNERS * CAP, dtype=jnp.int32)
    matched = places[:, None] == target[None, :]
    source = jnp.sum(jnp.where(matched, numbers[None, :], 0), axis=1)
    gradient = grad_parts[0]
    pieces = [
        lax.dynamic_slice(
            gradient, (0, 0, lax.rem(place + k, REP) * columns), (blocks, rows, columns)
        )
        for k in range(REP)
    ]
    terms, passing = sum_over_rep(pieces)
    rights = gather_over_rep(right_root[0], *passing)
    low, packed = sum_pack(source, terms)
    owned = exchange(packed)
    adam = lax.psum(adam_squares(low, moment), "rep")

    def spread(sent):
        return [sent[0]] + [shift(sent[k], k) for k in (1, 2, 3)]

    sent = left_multiply(place_ref, owned, left_root[0], 0, CAP)
    middle = sent.shape[2] // 2
    passed_right = shift(sent[2, :, :middle], 1)
    passed_left = shift(sent[2, :, middle:], 3)
    held = [sent[0], shift(sent[1], 1), None, None, shift(sent[3], 3)]
    held[2], held[3] = shift(passed_right, 1), shift(passed_left, 3)
    result, square = right_multiply(place_ref, held, rights)
    back = exchange(result)
    squares = lax.psum(jnp.sum(square, axis=(1, 2)), "rep")
    known = jnp.concatenate([adam, squares, jnp.zeros((128 - blocks - CAP,), jnp.float32)])
    known = jnp.broadcast_to(known[None, None, :], (OWNERS, 1, 128))
    sent = split_blocks(owner, slot, back)
    known = exchange(after(known, sent))[:, 0]
    adam_norm = jnp.sqrt(jnp.sum(known[:, :blocks], axis=0))
    by_place = jnp.transpose(known[:, blocks : blocks + CAP]).reshape(OWNERS * CAP, 1)
    shampoo_norm = jnp.sqrt(jnp.sum(jnp.where(matched, by_place, 0.0), axis=0))
    ratio = adam_norm / (shampoo_norm + norm_epsilon)
    held = spread(sent)
    return join_blocks(place_ref, ratio, held)


def solution(mesh):
    in_specs = (
        P("rep", None, "fsdp", None),
        P(None, "fsdp", "rep"),
        P(),
        P("fsdp", None, None, None),
        P("fsdp", None, None, "rep"),
    )
    out_specs = P(None, "fsdp", "rep")
    return jax.shard_map(shards, mesh=mesh, in_specs=in_specs, out_specs=out_specs, check_vma=False)
```

```python
import jax
import jax.numpy as jnp
from jax import lax
from jax.experimental import pallas as pl
from jax.experimental.pallas import tpu as pltpu
from jax.sharding import PartitionSpec as P

second_decay = 0.99
adam_epsilon = 1e-08
norm_epsilon = 1e-06

REP = 4
OWNERS = 64
CAP = 3
VMEM = pl.BlockSpec(memory_space=pltpu.VMEM)
SMEM = pl.BlockSpec(memory_space=pltpu.SMEM)
ROOM = 48 * 1024 * 1024


def block_slots(owner):
    count = owner.shape[0]
    numbers = jnp.arange(count, dtype=jnp.int32)
    same = owner[:, None] == owner[None, :]
    earlier = numbers[None, :] < numbers[:, None]
    return jnp.sum(jnp.where(same & earlier, 1, 0), axis=1).astype(jnp.int32)


def shift(value, step):
    return lax.ppermute(value, "rep", [(i, (i + step) % REP) for i in range(REP)])


def wide(value):
    return value.astype(jnp.float32)


def sum_over_rep(pieces):
    middle = pieces[0].shape[0] // 2
    top, bottom = slice(0, middle), slice(middle, None)
    far_right = shift(pieces[2][top], 1)
    far_left = shift(pieces[2][bottom], 3)
    near_right = shift(pieces[1][bottom], 1)
    near_left = shift(pieces[3][top], 3)
    on_right = (wide(pieces[1][top]) + wide(far_right)).astype(jnp.bfloat16)
    on_left = (wide(pieces[3][bottom]) + wide(far_left)).astype(jnp.bfloat16)
    last_right = shift(on_right, 1)
    last_left = shift(on_left, 3)
    return (pieces[0], near_left, last_right, near_right, last_left), (on_right, on_left)


def gather_over_rep(value, *others):
    middle = value.shape[1] // 2
    top, bottom = after((value[:, :middle], value[:, middle:]), *others)
    left_top = shift(top, 1)
    right_bottom = shift(bottom, 3)
    left_bottom = shift(bottom, 1)
    right_top = shift(top, 3)
    far_top = shift(left_top, 1)
    far_bottom = shift(right_bottom, 3)
    return value, left_top, left_bottom, far_top, far_bottom, right_top, right_bottom


def sum_pack_kernel(source, own, near_left, last_right, near_right, last_left, low, out):
    middle = near_left.shape[0]

    @pl.loop(0, middle, unroll=4)
    def _(b):
        low[b] = (wide(own[b]) + (wide(near_left[b]) + wide(last_right[b]))).astype(jnp.bfloat16)
        c = middle + b
        low[c] = (wide(own[c]) + (wide(near_right[b]) + wide(last_left[b]))).astype(jnp.bfloat16)

    @pl.loop(0, OWNERS, unroll=4)
    def _(o):
        for s in range(CAP):
            out[o, s] = low[source[s * OWNERS + o]]


def sum_pack(source, terms):
    blocks, rows, columns = terms[0].shape
    return pl.pallas_call(
        sum_pack_kernel,
        out_shape=[
            jax.ShapeDtypeStruct((blocks, rows, columns), jnp.bfloat16),
            jax.ShapeDtypeStruct((OWNERS, CAP, rows, columns), jnp.bfloat16),
        ],
        in_specs=[SMEM] + [VMEM] * 5,
        out_specs=[VMEM, VMEM],
        compiler_params=pltpu.CompilerParams(vmem_limit_bytes=ROOM),
        name="sum_pack",
    )(source, *terms)


def order_kernel(order, left, out):
    out[0] = jnp.dot(order[...], left[0], preferred_element_type=jnp.float32).astype(jnp.bfloat16)


def order_rows(left, rows):
    slots, size, _ = left.shape
    part = rows // REP
    number = jnp.arange(size, dtype=jnp.int32)
    target, j, o = number // (part * OWNERS), number // OWNERS % part, number % OWNERS
    taken = o * rows + target * part + j
    order = jnp.where(taken[:, None] == number[None, :], 1.0, 0.0).astype(jnp.bfloat16)
    return pl.pallas_call(
        order_kernel,
        grid=(slots,),
        out_shape=jax.ShapeDtypeStruct(left.shape, jnp.bfloat16),
        in_specs=[VMEM, pl.BlockSpec((1, size, size), lambda i: (i, 0, 0))],
        out_specs=pl.BlockSpec((1, size, size), lambda i: (i, 0, 0)),
        compiler_params=pltpu.CompilerParams(vmem_limit_bytes=ROOM),
        cost_estimate=pl.CostEstimate(
            flops=slots * 2 * size**3, bytes_accessed=slots * 4 * size * size, transcendentals=0
        ),
        name="order_rows",
    )(order, left)


def left_kernel(place, gradient, left, out):
    size = left.shape[1]
    width = gradient.shape[3]
    tile = size // REP
    low = gradient[:, pl.program_id(0)].reshape(size, width)
    for target in range(REP):
        k = lax.rem(target + REP - place[0], REP)
        rows = left[0, target * tile : (target + 1) * tile, :]
        product = jnp.dot(rows, low, preferred_element_type=jnp.float32)
        out[k, 0] = product.astype(jnp.bfloat16)


def left_multiply(place, gradient, left):
    count, size, _ = left.shape
    width = gradient.shape[3]
    return pl.pallas_call(
        left_kernel,
        grid=(count,),
        out_shape=jax.ShapeDtypeStruct((REP, count, size // REP, width), jnp.bfloat16),
        in_specs=[SMEM, VMEM, pl.BlockSpec((1, size, size), lambda i: (i, 0, 0))],
        out_specs=pl.BlockSpec((REP, 1, size // REP, width), lambda i: (0, i, 0, 0)),
        compiler_params=pltpu.CompilerParams(vmem_limit_bytes=ROOM),
        cost_estimate=pl.CostEstimate(
            flops=count * 2 * size * size * width,
            bytes_accessed=count * 4 * size * size,
            transcendentals=0,
        ),
        name="left_multiply",
    )(place, gradient, left)


def right_kernel(place, *refs):
    pieces, rights = refs[:REP], refs[REP : REP + 7]
    out, total, full, wide_rows = refs[REP + 7 :]
    height, size = full.shape
    width = size // REP
    halves, _, half = wide_rows.shape
    rows = out.shape[2]
    part = rows // REP
    for k, piece in enumerate(pieces):
        at = pl.multiple_of(lax.rem(place[0] + (REP - k), REP) * width, width)
        full[:, pl.ds(at, width)] = piece[0]
    squares = jnp.zeros((8, width), jnp.float32)
    middle = size // 2
    for k in range(REP):
        if k == 0:
            product = jnp.dot(full[...], rights[0][0], preferred_element_type=jnp.float32)
        else:
            top, bottom = rights[2 * k - 1], rights[2 * k]
            product = jnp.dot(full[:, :middle], top[0], preferred_element_type=jnp.float32)
            product = product + jnp.dot(
                full[:, middle:], bottom[0], preferred_element_type=jnp.float32
            )
        squares = squares + jnp.sum((product * product).reshape(height // 8, 8, width), axis=0)
        for j in range(part):
            for h in range(halves):
                wide_rows[h, pl.ds(k * part + j, OWNERS, stride=rows), :] = product[
                    j * OWNERS : (j + 1) * OWNERS, h * half : (h + 1) * half
                ]
    for h in range(halves):
        low = wide_rows[h].astype(jnp.bfloat16).reshape(OWNERS, rows, half)
        out[:, 0, :, h * half : (h + 1) * half] = low
    total[0] = jnp.sum(squares, axis=0, keepdims=True)


def right_multiply(place, pieces, rights):
    count, height, width = pieces[0].shape
    size = rights[0].shape[1]
    rows = size // OWNERS
    return pl.pallas_call(
        right_kernel,
        grid=(count,),
        out_shape=[
            jax.ShapeDtypeStruct((OWNERS, count, rows, width), jnp.bfloat16),
            jax.ShapeDtypeStruct((count, 1, width), jnp.float32),
        ],
        in_specs=[SMEM]
        + [pl.BlockSpec((1, height, width), lambda i: (i, 0, 0))] * 4
        + [pl.BlockSpec((1,) + r.shape[1:], lambda i: (i, 0, 0)) for r in rights],
        out_specs=[
            pl.BlockSpec((OWNERS, 1, rows, width), lambda i: (0, i, 0, 0)),
            pl.BlockSpec((1, 1, width), lambda i: (i, 0, 0)),
        ],
        scratch_shapes=[
            pltpu.VMEM((height, size), jnp.bfloat16),
            pltpu.VMEM((width // 128, size, 128), jnp.float32),
        ],
        compiler_params=pltpu.CompilerParams(vmem_limit_bytes=ROOM),
        cost_estimate=pl.CostEstimate(
            flops=count * 2 * size * size * width,
            bytes_accessed=count * 4 * size * size,
            transcendentals=0,
        ),
        name="right_multiply",
    )(place, *pieces, *rights)


def split_kernel(owner, slot, back, out):
    _, groups, rows, _ = out.shape
    part = rows // REP

    @pl.loop(0, groups, unroll=2)
    def _(g):
        parts = []
        for i in range(REP):
            b = g * REP + i
            parts.append(wide(back[owner[b], slot[b]]))
        for k in range(REP):
            joined = [p[k * part : (k + 1) * part] for p in parts]
            out[(REP - k) % REP, g] = jnp.concatenate(joined, axis=0).astype(jnp.bfloat16)


def split_blocks(owner, slot, back):
    blocks = owner.shape[0]
    _, _, rows, width = back.shape
    return pl.pallas_call(
        split_kernel,
        out_shape=jax.ShapeDtypeStruct((REP, blocks // REP, rows, width), jnp.bfloat16),
        in_specs=[SMEM] * 2 + [VMEM],
        out_specs=VMEM,
        compiler_params=pltpu.CompilerParams(vmem_limit_bytes=ROOM),
        name="split_blocks",
    )(owner, slot, back)


def join_kernel(place, ratio, own, first, second, third, out, held):
    groups, rows, _ = own.shape
    part = rows // REP
    for k, piece in enumerate((own, first, second, third)):
        held[lax.rem(place[0] + (REP - k), REP)] = piece[...]

    @pl.loop(0, groups, unroll=2)
    def _(g):
        parts = [wide(held[q, g]) for q in range(REP)]
        for i in range(REP):
            joined = [p[i * part : (i + 1) * part] for p in parts]
            out[g * REP + i] = jnp.concatenate(joined, axis=0) * ratio[g * REP + i]


def join_blocks(place, ratio, pieces):
    groups, rows, width = pieces[0].shape
    return pl.pallas_call(
        join_kernel,
        out_shape=jax.ShapeDtypeStruct((groups * REP, rows, width), jnp.float32),
        in_specs=[SMEM] * 2 + [VMEM] * 4,
        out_specs=VMEM,
        scratch_shapes=[pltpu.VMEM((REP, groups, rows, width), jnp.bfloat16)],
        compiler_params=pltpu.CompilerParams(vmem_limit_bytes=ROOM),
        name="join_blocks",
    )(place, ratio, *pieces)


def adam_squares(low, moment):
    gradient = wide(low)
    second = second_decay * moment + (1.0 - second_decay) * gradient * gradient
    direction = gradient / (jnp.sqrt(second) + adam_epsilon)
    return jnp.sum(direction * direction, axis=(1, 2))


def exchange(value):
    return lax.all_to_all(value, "fsdp", split_axis=0, concat_axis=0)


def after(value, *others):
    return lax.optimization_barrier((value, *others))[0]


def shards(grad_parts, moment, owner, left_root, right_root):
    place = lax.axis_index("rep")
    place_ref = place.astype(jnp.int32).reshape(1)
    blocks, rows, columns = moment.shape
    slot = block_slots(owner)
    numbers = jnp.arange(blocks, dtype=jnp.int32)
    target = slot * OWNERS + owner
    places = jnp.arange(OWNERS * CAP, dtype=jnp.int32)
    matched = places[:, None] == target[None, :]
    source = jnp.sum(jnp.where(matched, numbers[None, :], 0), axis=1)
    gradient = grad_parts[0]
    pieces = [
        lax.dynamic_slice(
            gradient, (0, 0, lax.rem(place + k, REP) * columns), (blocks, rows, columns)
        )
        for k in range(REP)
    ]
    terms, passing = sum_over_rep(pieces)
    rights = gather_over_rep(right_root[0], *passing)
    low, packed = sum_pack(source, terms)
    owned = exchange(packed)
    ordered = order_rows(left_root[0], rows)
    adam = lax.psum(adam_squares(low, moment), "rep")

    def spread(sent):
        return [sent[0]] + [shift(sent[k], k) for k in (1, 2, 3)]

    held = spread(left_multiply(place_ref, owned, ordered))
    result, square = right_multiply(place_ref, held, rights)
    back = exchange(result)
    squares = lax.psum(jnp.sum(square, axis=(1, 2)), "rep")
    known = jnp.concatenate([adam, squares, jnp.zeros((128 - blocks - CAP,), jnp.float32)])
    known = jnp.broadcast_to(known[None, None, :], (OWNERS, 1, 128))
    sent = split_blocks(owner, slot, back)
    known = exchange(after(known, sent))[:, 0]
    adam_norm = jnp.sqrt(jnp.sum(known[:, :blocks], axis=0))
    by_place = jnp.transpose(known[:, blocks : blocks + CAP]).reshape(OWNERS * CAP, 1)
    shampoo_norm = jnp.sqrt(jnp.sum(jnp.where(matched, by_place, 0.0), axis=0))
    ratio = adam_norm / (shampoo_norm + norm_epsilon)
    held = spread(sent)
    return join_blocks(place_ref, ratio, held)


def solution(mesh):
    in_specs = (
        P("rep", None, "fsdp", None),
        P(None, "fsdp", "rep"),
        P(),
        P("fsdp", None, None, None),
        P("fsdp", None, None, "rep"),
    )
    out_specs = P(None, "fsdp", "rep")
    return jax.shard_map(shards, mesh=mesh, in_specs=in_specs, out_specs=out_specs, check_vma=False)
```
